32 devices in a mesh: ctx: 4 (over y, x), chan: 8 (over z, core).
Axes of the slice: x: 2, y: 2, z: 4, core: 2. Of those that a mesh axis runs over, the one named last changes fastest.
Arguments:
- featurized: bfloat16 [8192, 3, 8192], P('ctx', None, 'chan'), may hold values from -6 to 6
- short_filter: float32 [3, 3, 8192], P(None, None, 'chan'), may hold values from -2.5 to 2.5
- decay_rate: float32 [512, 16], P('chan'), as said below
- residue: float32 [512, 16], P('chan'), may hold values from -2.5 to 2.5
- skip_gain: float32 [8192], P('chan'), may hold values from 0.25 to 1.5
- out_weight: bfloat16 [8192, 4096], P('chan'), may hold values from -0.0625 to 0.0625
Outputs:
- output: bfloat16 [8192, 4096], P(('ctx', 'chan'))
The draws below stay inside these ranges and needn't reach their ends.
Inputs may be any that keep to these rules, and one draw needn't show every extreme that they name: `decay_rate`: each rate is at least 0.2 / 8192.
All inputs are finite; a program needn't handle non-finite values.
Results may differ from the reference program's by a relative error of at most 0.02.
Values may be sent and summed in bfloat16 or wider, within the bound.
No kernel may reach another device: no remote copies, remote signals or barrier semaphores. Data moves between devices by JAX's collectives and lax.ppermute only.
A program may use at most 320 MiB of HBM per device.

```python
import math
import jax
import jax.numpy as jnp
from jax import lax

D = 8192
FGROUP = 16
MODES = 16
OUTC = 4096
LENGTH = 8192
N_CHAN = 8


def draw_decay_rate(key, part):
    filter_count = D // FGROUP
    subkeys = jax.random.split(key, 3)
    slow_share = 0.5
    slow_pick = jax.random.uniform(subkeys[0], (filter_count, MODES)) < slow_share
    fast_rate = jnp.exp(jax.random.uniform(subkeys[1], (filter_count, MODES), minval=math.log(1.0 / 50.0), maxval=math.log(1.0 / 20.0)))
    slow_rate = jnp.exp(jax.random.uniform(subkeys[2], (filter_count, MODES), minval=math.log(0.2), maxval=math.log(1.5))) / LENGTH
    return jnp.where(slow_pick, slow_rate, fast_rate).astype(jnp.float32)


def steps_of(own_key, dims, cuts, low, largest):
    def one(position, parts):
        draws = jax.random.uniform(jax.random.fold_in(jax.random.fold_in(own_key, 6), position), (parts,), jnp.float32, low / len(cuts), largest / len(cuts))
        return jnp.repeat(jnp.exp(draws), dims[position] // parts).reshape((-1,) + (1,) * (len(dims) - position - 1))

    factor_of = one(*cuts[0])
    for cut in cuts[1:]:
        factor_of = factor_of * one(*cut)
    return factor_of


def gaussian(key, shape, spread, reach, pieces=(), kind=jnp.bfloat16):
    level = steps_of(key, shape, pieces, -0.22, 0.18) if pieces else 1.0
    array = jax.random.normal(key, shape, jnp.float32) * spread * level
    return jnp.minimum(jnp.maximum(array, -reach), reach).astype(kind)


def setup_inputs(seed: int = 0) -> dict:
    key_list = jax.random.split(jax.random.key(seed), 7)
    return {
        "featurized": gaussian(key_list[0], (LENGTH, 3, D), 1.0, 6.0, ((0, 4), (2, 8))),
        "short_filter": gaussian(key_list[1], (3, 3, D), 0.5, 2.5, ((2, 8),), jnp.float32),
        "decay_rate": draw_decay_rate(jax.random.fold_in(key_list[6], 71), 0),
        "residue": gaussian(key_list[3], (D // FGROUP, MODES), 0.5, 2.5, ((0, 8),), jnp.float32),
        "skip_gain": jnp.clip(0.25 + 1.25 * jax.random.uniform(key_list[4], (D,), jnp.float32) ** steps_of(key_list[4], (D,), ((0, 8),), -0.2, 0.2), 0.25, 1.5),
        "out_weight": gaussian(key_list[5], (D, OUTC), D ** -0.5, 0.0625, ((0, 8),)),
    }


def reference(featurized, short_filter, decay_rate, residue, skip_gain, out_weight):
    inputs = featurized.astype(jnp.float32)
    padded = jnp.pad(inputs, ((2, 0), (0, 0), (0, 0)))
    shortened = short_filter[0] * padded[2:] + short_filter[1] * padded[1:-1] + short_filter[2] * padded[:-2]
    query_part = shortened[:, 0]
    gated = (shortened[:, 1] * shortened[:, 2]).astype(jnp.bfloat16)
    gated_float = gated.astype(jnp.float32)
    seq_length = gated.shape[0]
    filter_count = decay_rate.shape[0]
    scaled = residue * jnp.sqrt(-jnp.expm1(-2.0 * decay_rate))
    lags = jnp.arange(seq_length, dtype=jnp.float32)
    fft_len = 2 * seq_length
    signals = gated_float.reshape(seq_length, filter_count, FGROUP).transpose(1, 2, 0)

    def one_filter(triple):
        rates, weights, rows = triple
        kernel = lax.optimization_barrier(jnp.sum(weights[:, None] * jnp.exp(-rates[:, None] * lags[None, :]), axis=0))
        spectrum = jnp.fft.rfft(rows, n=fft_len, axis=1) * jnp.fft.rfft(kernel, n=fft_len)[None, :]
        return jnp.fft.irfft(spectrum, n=fft_len, axis=1)[:, :seq_length]
    convolved = lax.map(one_filter, (decay_rate, scaled, signals))
    long_conv = convolved.transpose(2, 0, 1).reshape(seq_length, D)
    mixed_rows = (query_part * (long_conv + skip_gain * gated_float)).astype(jnp.bfloat16)
    group_cols = D // N_CHAN
    grouped = mixed_rows.reshape(seq_length, N_CHAN, group_cols).transpose(1, 0, 2)
    weights = out_weight.reshape(N_CHAN, group_cols, OUTC)

    def add_group(summed, group_pair):
        rows_part, weight_part = group_pair
        partial_value = jnp.dot(rows_part.astype(jnp.float32), weight_part.astype(jnp.float32), preferred_element_type=jnp.float32)
        rounded = lax.optimization_barrier(partial_value.astype(jnp.bfloat16))
        return (summed + rounded.astype(jnp.float32), None)
    summed_all, unused = lax.scan(add_group, jnp.zeros((seq_length, OUTC), jnp.float32), (grouped, weights))
    return summed_all.astype(jnp.bfloat16)
```

```python
import functools

import jax
import jax.numpy as jnp
from jax import lax
from jax.experimental import pallas as pl
from jax.experimental.pallas import tpu as pltpu
from jax.sharding import PartitionSpec as P

LANES = 128
CHUNK = 128
BF16 = jnp.bfloat16
F32 = jnp.float32


def params(mib=48):
    return pltpu.CompilerParams(vmem_limit_bytes=mib << 20)


def cost(flops, moved):
    return pl.CostEstimate(flops=int(flops), bytes_accessed=int(moved), transcendentals=0)


def iota(shape, dim):
    return lax.broadcasted_iota(jnp.int32, shape, dim)


def toeplitz_kernel(modes, rate_ref, scale_ref, tile_ref):
    filters = LANES // modes
    reach = iota((LANES, CHUNK), 1).astype(F32)
    terms = scale_ref[...] * jnp.exp(-rate_ref[...] * reach)
    taps = terms.reshape(filters, modes, CHUNK).sum(axis=1)
    keep = iota((CHUNK, CHUNK), 0) <= iota((CHUNK, CHUNK), 1)
    for f in range(filters):
        rows = jnp.broadcast_to(taps[f : f + 1], (CHUNK, CHUNK))
        rolled = pltpu.roll(rows, 0, 1, stride=1, stride_axis=0)
        tile_ref[f] = jnp.where(keep, rolled, 0.0).astype(BF16)


def short_conv(stream, stage_ref, x_ref, rim_ref, taps_ref, k):
    at = 8 + k * CHUNK
    return (
        taps_ref[0, stream : stream + 1, :] * stage_ref[at : at + CHUNK, :]
        + taps_ref[1, stream : stream + 1, :] * stage_ref[at - 1 : at - 1 + CHUNK, :]
        + taps_ref[2, stream : stream + 1, :] * stage_ref[at - 2 : at - 2 + CHUNK, :]
    )


def stage(stream, stage_ref, x_ref, rim_ref):
    stage_ref[0:8, :] = jnp.zeros((8, LANES), F32)
    stage_ref[6:8, :] = rim_ref[stream].astype(F32)
    stage_ref[8:, :] = x_ref[0].astype(F32)


def diagonal(modes, group):
    return (iota((LANES, LANES), 0) // modes) == (iota((LANES, LANES), 1) // group)


def dot(a, b, dims=((1,), (0,))):
    return lax.dot_general(a, b, (dims, ((), ())), preferred_element_type=F32)


def gate_kernel(modes, group, k_ref, v_ref, rim_ref, taps_ref, rate_ref, gated_ref, state_ref, k_stage, v_stage):
    stage(1, k_stage, k_ref, rim_ref)
    stage(2, v_stage, v_ref, rim_ref)
    rate = rate_ref[...]
    ends = jnp.exp(-rate * (CHUNK - 1 - iota((LANES, CHUNK), 1)).astype(F32)).astype(BF16)
    fade = jnp.exp(-rate * CHUNK)
    state = jnp.zeros((LANES, LANES), F32)
    for k in range(gated_ref.shape[0] // CHUNK):
        gated = (
            short_conv(1, k_stage, k_ref, rim_ref, taps_ref, k) * short_conv(2, v_stage, v_ref, rim_ref, taps_ref, k)
        ).astype(BF16)
        gated_ref[k * CHUNK : (k + 1) * CHUNK, :] = gated
        state = fade * state + dot(ends, gated)
    state = jnp.where(diagonal(modes, group), state, 0.0).astype(BF16)
    fold = (iota((group, LANES), 0) == lax.rem(iota((group, LANES), 1), group)).astype(BF16)
    state_ref[...] = dot(fold, state, ((1,), (1,))).astype(BF16)


def near_kernel(
    modes,
    group,
    gated_ref,
    tile_ref,
    q_ref,
    rim_ref,
    taps_ref,
    gain_ref,
    row_rate_ref,
    row_scale_ref,
    near_ref,
    query_ref,
    q_stage,
    sources,
    sums,
):
    stage(0, q_stage, q_ref, rim_ref)
    filters = LANES // group
    chunks = gated_ref.shape[0] // CHUNK
    eye = (iota((CHUNK, CHUNK), 0) == iota((CHUNK, CHUNK), 1)).astype(BF16)
    for k in range(0, chunks, 2):
        turned = dot(eye, gated_ref[k * CHUNK : (k + 2) * CHUNK, :], ((1,), (1,))).astype(BF16)
        sources[k] = turned[:, :CHUNK]
        sources[k + 1] = turned[:, CHUNK:]
    for f in range(filters):
        rows = slice(f * group, (f + 1) * group)
        block = sources[:, rows, :].reshape(chunks * group, CHUNK)
        sums[:, rows, :] = dot(block, tile_ref[f]).astype(BF16).reshape(chunks, group, CHUNK)
    row_rate = row_rate_ref[0]
    ends = jnp.exp(-row_rate * (CHUNK - 1 - iota((CHUNK, LANES), 0)).astype(F32)).astype(BF16)
    reads = (row_scale_ref[0] * jnp.exp(-row_rate * (iota((CHUNK, LANES), 0) + 1).astype(F32))).astype(BF16)
    both = jnp.concatenate([eye, reads], axis=1)
    fade = jnp.exp(-row_rate * CHUNK)
    own_modes = diagonal(group, modes)
    gain = gain_ref[...]
    state = jnp.zeros((LANES, LANES), F32)
    for k in range(chunks):
        rows = slice(k * CHUNK, (k + 1) * CHUNK)
        summed = dot(both, jnp.concatenate([sums[k], state.astype(BF16)], axis=1), ((1,), (1,)))
        state = fade * state + jnp.where(own_modes, dot(sources[k], ends), 0.0)
        near_ref[rows, :] = (summed + gain * gated_ref[rows, :].astype(F32)).astype(BF16)
        query_ref[rows, :] = short_conv(0, q_stage, q_ref, rim_ref, taps_ref, k).astype(BF16)


def mix_kernel(modes, group, parts, core_ref, near_ref, query_ref, *rest):
    *piece_refs, row_rate_ref, row_scale_ref, keep_ref, give_ref, mixed_ref = rest
    tok_rows = near_ref.shape[0]
    size = tok_rows // (2 * parts)
    core = core_ref[0]
    row_rate = row_rate_ref[0]
    carried = jnp.zeros((group, LANES), F32)
    for d, piece_ref in enumerate(piece_refs):
        carried = carried + jnp.exp(-row_rate * float(d * tok_rows)) * piece_ref[...].astype(F32)
    state = jnp.where(diagonal(group, modes), jnp.concatenate([carried] * (LANES // group), axis=0), 0.0).astype(BF16)
    reads = row_scale_ref[0] * jnp.exp(-row_rate * (iota((CHUNK, LANES), 0) + 1).astype(F32))
    for k in range(tok_rows // CHUNK):
        rows = slice(k * CHUNK, (k + 1) * CHUNK)
        fade = jnp.exp(-row_rate * float(k * CHUNK))
        far = dot((reads * fade).astype(BF16), state, ((1,), (1,)))
        mixed = (query_ref[rows, :].astype(F32) * (near_ref[rows, :].astype(F32) + far)).astype(BF16)
        width = min(size, CHUNK)
        for piece in range(0, CHUNK, width):
            block, inner = divmod(k * CHUNK + piece, size)
            side = lax.rem(core + block, 2)
            mixed_ref[side, block // 2, inner : inner + width, :] = mixed[piece : piece + width]
    keep_ref[...] = mixed_ref[0]
    give_ref[...] = mixed_ref[1]


def product_kernel(which_ref, own_ref, other_ref, own_w_ref, other_w_ref, out_ref):
    out_ref[...] = (dot(own_ref[0], own_w_ref[...]) + dot(other_ref[0], other_w_ref[...])).astype(BF16)


def product(which, own, other, own_w, other_w, part, split):
    _, rows, depth = own.shape
    width = own_w.shape[1] // split
    tile = min(512, width)
    steps = width // tile
    grid_spec = pltpu.PrefetchScalarGridSpec(
        num_scalar_prefetch=1,
        grid=(steps,),
        in_specs=[
            pl.BlockSpec((1, rows, depth), lambda j, which: (which[0], 0, 0)),
            pl.BlockSpec((1, rows, depth), lambda j, which: (which[0], 0, 0)),
            pl.BlockSpec((depth, tile), lambda j, which: (0, part * steps + j)),
            pl.BlockSpec((depth, tile), lambda j, which: (0, part * steps + j)),
        ],
        out_specs=pl.BlockSpec((rows, tile), lambda j, which: (0, j)),
    )
    return pl.pallas_call(
        product_kernel,
        grid_spec=grid_spec,
        out_shape=jax.ShapeDtypeStruct((rows, width), BF16),
        compiler_params=params(),
        cost_estimate=cost(4 * rows * depth * width, 4 * depth * width + 6 * rows * width),
        name="product",
    )(which.reshape(1).astype(jnp.int32), own, other, own_w, other_w)


def shifted(value, axis, steps):
    count = lax.axis_size(axis)
    return lax.ppermute(value, axis, [(i, i + steps) for i in range(count - steps)])


def on_device(featurized, short_filter, decay_rate, residue, skip_gain, out_weight):
    tok_rows, streams, channels = featurized.shape
    filters, modes = decay_rate.shape
    group = channels // filters
    blocks = channels // LANES
    ctx_count = lax.axis_size("ctx")
    parts = lax.axis_size("chan") // 2
    chan_index = lax.axis_index("chan")
    place, core = chan_index // 2, chan_index % 2
    swap = [(i, i ^ 1) for i in range(2 * parts)]

    rim = shifted(featurized[tok_rows - 2 :], "ctx", 1).transpose(1, 0, 2)
    other_weight = lax.ppermute(out_weight, "chan", swap)
    features = featurized.transpose(1, 0, 2)
    scaled = residue * jnp.sqrt(-jnp.expm1(-2.0 * decay_rate))
    rate_cols = jnp.broadcast_to(decay_rate.reshape(-1, 1), (filters * modes, LANES))
    scale_cols = jnp.broadcast_to(scaled.reshape(-1, 1), (filters * modes, LANES))
    rate_rows = decay_rate.reshape(blocks, 1, LANES)
    scale_rows = scaled.reshape(blocks, 1, LANES)
    per_block = LANES // group

    square = pl.BlockSpec((LANES, LANES), lambda g: (g, 0))
    tile_spec = pl.BlockSpec((per_block, CHUNK, CHUNK), lambda g: (g, 0, 0))
    lanes_spec = pl.BlockSpec((tok_rows, LANES), lambda g: (0, g))
    rim_spec = pl.BlockSpec((streams, 2, LANES), lambda g: (0, 0, g))
    taps_spec = pl.BlockSpec((3, streams, LANES), lambda g: (0, 0, g))
    state_spec = pl.BlockSpec((group, LANES), lambda g: (g, 0))

    def stream_spec(i):
        return pl.BlockSpec((1, tok_rows, LANES), lambda g: (i, 0, g))

    tiles = pl.pallas_call(
        functools.partial(toeplitz_kernel, modes),
        grid=(blocks,),
        in_specs=[square, square],
        out_specs=tile_spec,
        out_shape=jax.ShapeDtypeStruct((filters, CHUNK, CHUNK), BF16),
        compiler_params=params(),
        cost_estimate=cost(filters * CHUNK * CHUNK * 40, filters * CHUNK * CHUNK * 4),
        name="toeplitz",
    )(rate_cols, scale_cols)

    stage_shape = pltpu.VMEM((8 + tok_rows, LANES), F32)
    wide = jax.ShapeDtypeStruct((tok_rows, channels), BF16)
    gated, state = pl.pallas_call(
        functools.partial(gate_kernel, modes, group),
        grid=(blocks,),
        in_specs=[stream_spec(1), stream_spec(2), rim_spec, taps_spec, square],
        out_specs=[lanes_spec, state_spec],
        out_shape=[wide, jax.ShapeDtypeStruct((blocks * group, LANES), BF16)],
        scratch_shapes=[stage_shape, stage_shape],
        compiler_params=params(),
        cost_estimate=cost(tok_rows * channels * 256, tok_rows * channels * 6),
        name="gate",
    )(features, features, rim, short_filter, rate_cols)

    pieces = [shifted(state, "ctx", d) for d in range(1, ctx_count)]

    row_spec = pl.BlockSpec((1, 1, LANES), lambda g: (g, 0, 0))
    chunks = tok_rows // CHUNK
    near, query = pl.pallas_call(
        functools.partial(near_kernel, modes, group),
        grid=(blocks,),
        in_specs=[
            lanes_spec,
            tile_spec,
            stream_spec(0),
            rim_spec,
            taps_spec,
            pl.BlockSpec((1, LANES), lambda g: (0, g)),
            row_spec,
            row_spec,
        ],
        out_specs=[lanes_spec, lanes_spec],
        out_shape=[wide, wide],
        scratch_shapes=[
            stage_shape,
            pltpu.VMEM((chunks, LANES, CHUNK), BF16),
            pltpu.VMEM((chunks, LANES, CHUNK), BF16),
        ],
        compiler_params=params(),
        cost_estimate=cost(tok_rows * channels * 1024, tok_rows * channels * 8),
        name="near",
    )(gated, tiles, features, rim, short_filter, skip_gain.reshape(1, channels), rate_rows, scale_rows)

    size = tok_rows // (2 * parts)
    out_spec = pl.BlockSpec((parts, size, LANES), lambda g, core: (0, 0, g))
    lanes_two = pl.BlockSpec((tok_rows, LANES), lambda g, core: (0, g))
    row_two = pl.BlockSpec((1, 1, LANES), lambda g, core: (g, 0, 0))
    part_shape = jax.ShapeDtypeStruct((parts, size, channels), BF16)
    keep, give = pl.pallas_call(
        functools.partial(mix_kernel, modes, group, parts),
        grid_spec=pltpu.PrefetchScalarGridSpec(
            num_scalar_prefetch=1,
            grid=(blocks,),
            in_specs=[lanes_two, lanes_two]
            + [pl.BlockSpec((group, LANES), lambda g, core: (g, 0))] * len(pieces)
            + [row_two, row_two],
            out_specs=[out_spec, out_spec],
            scratch_shapes=[pltpu.VMEM((2, parts, size, LANES), BF16)],
        ),
        out_shape=[part_shape, part_shape],
        compiler_params=params(),
        cost_estimate=cost(tok_rows * channels * 256, tok_rows * channels * 8),
        name="mix",
    )(core.reshape(1).astype(jnp.int32), near, query, *pieces, rate_rows, scale_rows)

    other = lax.ppermute(give, "chan", swap)

    split = 2
    last = parts - 1
    multiply = lambda which, j: product(jnp.clip(which, 0, last), keep, other, out_weight, other_weight, j, split)
    up = [None] * split
    down = [None] * split
    for s in range(1, parts):
        senders = range(0, min(s, last))
        up_pairs = [(2 * i + c, 2 * i + 2 + c) for i in senders for c in (0, 1)]
        down_pairs = [(2 * (last - i) + c, 2 * (last - i) - 2 + c) for i in senders for c in (0, 1)]
        for j in range(split):
            if s == 1:
                first = multiply(jnp.where(place == 0, last, 0), j)
                up[j], down[j] = first, first
            else:
                up[j] = (multiply(parts - s + place, j).astype(F32) + up[j].astype(F32)).astype(BF16)
                down[j] = (multiply(s - parts + place, j).astype(F32) + down[j].astype(F32)).astype(BF16)
            up[j] = lax.ppermute(up[j], "chan", up_pairs)
            down[j] = lax.ppermute(down[j], "chan", down_pairs)
    outs = [
        (multiply(place, j).astype(F32) + up[j].astype(F32) + down[j].astype(F32)).astype(BF16) for j in range(split)
    ]
    return jnp.concatenate(outs, axis=1)


def solution(mesh):
    return jax.shard_map(
        on_device,
        mesh=mesh,
        in_specs=(
            P("ctx", None, "chan"),
            P(None, None, "chan"),
            P("chan", None),
            P("chan", None),
            P("chan"),
            P("chan", None),
        ),
        out_specs=P(("ctx", "chan"), None),
        check_vma=False,
    )
```

```python
import functools

import jax
import jax.numpy as jnp
from jax import lax
from jax.experimental import pallas as pl
from jax.experimental.pallas import tpu as pltpu
from jax.sharding import PartitionSpec as P

LANES = 128
CHUNK = 128
BF16 = jnp.bfloat16
F32 = jnp.float32


def params(mib=48):
    return pltpu.CompilerParams(vmem_limit_bytes=mib << 20)


def cost(flops, moved):
    return pl.CostEstimate(flops=int(flops) // 64, bytes_accessed=int(moved) // 64, transcendentals=0)


def iota(shape, dim):
    return lax.broadcasted_iota(jnp.int32, shape, dim)


def toeplitz_kernel(modes, rate_ref, scale_ref, tile_ref):
    filters = LANES // modes
    reach = iota((LANES, CHUNK), 1).astype(F32)
    terms = scale_ref[...] * jnp.exp(-rate_ref[...] * reach)
    taps = terms.reshape(filters, modes, CHUNK).sum(axis=1)
    keep = iota((CHUNK, CHUNK), 0) <= iota((CHUNK, CHUNK), 1)
    for f in range(filters):
        rows = jnp.broadcast_to(taps[f : f + 1], (CHUNK, CHUNK))
        rolled = pltpu.roll(rows, 0, 1, stride=1, stride_axis=0)
        tile_ref[f] = jnp.where(keep, rolled, 0.0).astype(BF16)


def short_conv(stream, stage_ref, x_ref, rim_ref, taps_ref, k):
    at = 8 + k * CHUNK
    return (
        taps_ref[0, stream : stream + 1, :] * stage_ref[at : at + CHUNK, :]
        + taps_ref[1, stream : stream + 1, :] * stage_ref[at - 1 : at - 1 + CHUNK, :]
        + taps_ref[2, stream : stream + 1, :] * stage_ref[at - 2 : at - 2 + CHUNK, :]
    )


def stage(stream, stage_ref, x_ref, rim_ref):
    stage_ref[0:8, :] = jnp.zeros((8, LANES), F32)
    stage_ref[6:8, :] = rim_ref[stream].astype(F32)
    stage_ref[8:, :] = x_ref[0].astype(F32)


def diagonal(modes, group):
    return (iota((LANES, LANES), 0) // modes) == (iota((LANES, LANES), 1) // group)


def dot(a, b, dims=((1,), (0,))):
    return lax.dot_general(a, b, (dims, ((), ())), preferred_element_type=F32)


def gate_kernel(
    modes, group, k_ref, v_ref, rim_ref, taps_ref, rate_ref, gated_ref, start_ref, state_ref, k_stage, v_stage
):
    stage(1, k_stage, k_ref, rim_ref)
    stage(2, v_stage, v_ref, rim_ref)
    rate = rate_ref[...]
    ends = jnp.exp(-rate * (CHUNK - 1 - iota((LANES, CHUNK), 1)).astype(F32)).astype(BF16)
    fade = jnp.exp(-rate * CHUNK)
    state = jnp.zeros((LANES, LANES), F32)
    chunks = gated_ref.shape[0] // CHUNK
    per_block = chunks // start_ref.shape[0]
    own_modes = diagonal(modes, group)
    spots = (iota((group, LANES), 0) == lax.rem(iota((group, LANES), 1), group)).astype(BF16)
    fold = lambda value: dot(spots, jnp.where(own_modes, value, 0.0).astype(BF16), ((1,), (1,))).astype(BF16)
    for k in range(chunks):
        if k % per_block == 0:
            start_ref[k // per_block] = fold(state)
        gated = (
            short_conv(1, k_stage, k_ref, rim_ref, taps_ref, k) * short_conv(2, v_stage, v_ref, rim_ref, taps_ref, k)
        ).astype(BF16)
        gated_ref[k * CHUNK : (k + 1) * CHUNK, :] = gated
        state = fade * state + dot(ends, gated)
    state_ref[...] = fold(state)


def spread(modes, group, folded):
    return jnp.where(diagonal(group, modes), jnp.concatenate([folded] * (LANES // group), axis=0), 0.0)


def near_kernel(
    modes,
    group,
    window_ref,
    gated_ref,
    start_ref,
    tile_ref,
    q_ref,
    before_ref,
    rim_ref,
    taps_ref,
    gain_ref,
    row_rate_ref,
    row_scale_ref,
    *rest,
):
    near_ref, query_ref, q_stage, sources, sums = rest[-5:]

    stage(0, q_stage, q_ref, rim_ref)

    @pl.when(window_ref[0] > 0)
    def _():
        q_stage[6:8, :] = before_ref[0].astype(F32)[before_ref.shape[1] - 2 :]

    filters = LANES // group
    chunks = gated_ref.shape[0] // CHUNK
    eye = (iota((CHUNK, CHUNK), 0) == iota((CHUNK, CHUNK), 1)).astype(BF16)
    for k in range(0, chunks, 2):
        turned = dot(eye, gated_ref[k * CHUNK : (k + 2) * CHUNK, :], ((1,), (1,))).astype(BF16)
        sources[k] = turned[:, :CHUNK]
        sources[k + 1] = turned[:, CHUNK:]
    for f in range(filters):
        rows = slice(f * group, (f + 1) * group)
        block = sources[:, rows, :].reshape(chunks * group, CHUNK)
        sums[:, rows, :] = dot(block, tile_ref[f]).astype(BF16).reshape(chunks, group, CHUNK)
    row_rate = row_rate_ref[0]
    ends = jnp.exp(-row_rate * (CHUNK - 1 - iota((CHUNK, LANES), 0)).astype(F32)).astype(BF16)
    reads = (row_scale_ref[0] * jnp.exp(-row_rate * (iota((CHUNK, LANES), 0) + 1).astype(F32))).astype(BF16)
    both = jnp.concatenate([eye, reads], axis=1)
    fade = jnp.exp(-row_rate * CHUNK)
    own_modes = diagonal(group, modes)
    gain = gain_ref[...]
    state = spread(modes, group, start_ref[0].astype(F32))
    for k in range(chunks):
        rows = slice(k * CHUNK, (k + 1) * CHUNK)
        summed = dot(both, jnp.concatenate([sums[k], state.astype(BF16)], axis=1), ((1,), (1,)))
        state = fade * state + jnp.where(own_modes, dot(sources[k], ends), 0.0)
        near_ref[rows, :] = (summed + gain * gated_ref[rows, :].astype(F32)).astype(BF16)
        query_ref[rows, :] = short_conv(0, q_stage, q_ref, rim_ref, taps_ref, k).astype(BF16)


def mix_kernel(modes, group, tok_rows, size, where_ref, near_ref, query_ref, *rest):
    *piece_refs, row_rate_ref, row_scale_ref, keep_ref, give_ref, mixed_ref = rest
    core = where_ref[0]
    first = (where_ref[1] * near_ref.shape[0]).astype(F32)
    row_rate = row_rate_ref[0]
    carried = jnp.zeros((group, LANES), F32)
    for d, piece_ref in enumerate(piece_refs):
        carried = carried + jnp.exp(-row_rate * float(d * tok_rows)) * piece_ref[...].astype(F32)
    state = spread(modes, group, carried).astype(BF16)
    reads = row_scale_ref[0] * jnp.exp(-row_rate * (iota((CHUNK, LANES), 0) + 1).astype(F32))
    for k in range(near_ref.shape[0] // CHUNK):
        rows = slice(k * CHUNK, (k + 1) * CHUNK)
        fade = jnp.exp(-row_rate * (first + float(k * CHUNK)))
        far = dot((reads * fade).astype(BF16), state, ((1,), (1,)))
        mixed = (query_ref[rows, :].astype(F32) * (near_ref[rows, :].astype(F32) + far)).astype(BF16)
        width = min(size, CHUNK)
        for piece in range(0, CHUNK, width):
            block, inner = divmod(k * CHUNK + piece, size)
            side = lax.rem(core + block, 2)
            mixed_ref[side, block // 2, inner : inner + width, :] = mixed[piece : piece + width]
    keep_ref[...] = mixed_ref[0]
    give_ref[...] = mixed_ref[1]


def product_kernel(which_ref, own_ref, other_ref, own_w_ref, other_w_ref, out_ref):
    out_ref[...] = (dot(own_ref[0], own_w_ref[...]) + dot(other_ref[0], other_w_ref[...])).astype(BF16)


def product(which, own, other, own_w, other_w, part, split, other_which=None):
    _, rows, depth = own.shape
    width = own_w.shape[1] // split
    tile = min(1024, width)
    steps = width // tile
    grid_spec = pltpu.PrefetchScalarGridSpec(
        num_scalar_prefetch=1,
        grid=(steps,),
        in_specs=[
            pl.BlockSpec((1, rows, depth), lambda j, which: (which[0], 0, 0)),
            pl.BlockSpec((1, rows, depth), lambda j, which: (which[1], 0, 0)),
            pl.BlockSpec((depth, tile), lambda j, which: (0, part * steps + j)),
            pl.BlockSpec((depth, tile), lambda j, which: (0, part * steps + j)),
        ],
        out_specs=pl.BlockSpec((rows, tile), lambda j, which: (0, j)),
    )
    return pl.pallas_call(
        product_kernel,
        grid_spec=grid_spec,
        out_shape=jax.ShapeDtypeStruct((rows, width), BF16),
        compiler_params=params(),
        cost_estimate=cost(4 * rows * depth * width, 4 * depth * width + 6 * rows * width),
        name="product",
    )(jnp.stack([which, which if other_which is None else other_which]).astype(jnp.int32), own, other, own_w, other_w)


def shifted(value, axis, steps):
    count = lax.axis_size(axis)
    return lax.ppermute(value, axis, [(i, i + steps) for i in range(count - steps)])


def tie(*values):
    return lax.optimization_barrier(values)


def add(*values):
    total = values[0].astype(F32)
    for value in values[1:]:
        total = total + value.astype(F32)
    return total.astype(BF16)


def pairs(hops):
    return [(2 * i + c, 2 * j + c) for i, j in hops for c in (0, 1)]


def sum_over_line(place, keep, other, out_weight, other_weight):
    parts = keep.shape[0]
    split = 2
    last = parts - 1
    multiply = lambda which, j: product(jnp.clip(which, 0, last), keep, other, out_weight, other_weight, j, split)
    up = [None] * split
    down = [None] * split
    for s in range(1, parts):
        senders = range(0, min(s, last))
        up_pairs = [(2 * i + c, 2 * i + 2 + c) for i in senders for c in (0, 1)]
        down_pairs = [(2 * (last - i) + c, 2 * (last - i) - 2 + c) for i in senders for c in (0, 1)]
        for j in range(split):
            if s == 1:
                first = multiply(jnp.where(place == 0, last, 0), j)
                up[j], down[j] = first, first
            else:
                up[j] = (multiply(parts - s + place, j).astype(F32) + up[j].astype(F32)).astype(BF16)
                down[j] = (multiply(s - parts + place, j).astype(F32) + down[j].astype(F32)).astype(BF16)
            up[j] = lax.ppermute(up[j], "chan", up_pairs)
            down[j] = lax.ppermute(down[j], "chan", down_pairs)
    outs = [
        (multiply(place, j).astype(F32) + up[j].astype(F32) + down[j].astype(F32)).astype(BF16) for j in range(split)
    ]
    return jnp.concatenate(outs, axis=1)


def on_device(featurized, short_filter, decay_rate, residue, skip_gain, out_weight):
    tok_rows, streams, channels = featurized.shape
    filters, modes = decay_rate.shape
    group = channels // filters
    blocks = channels // LANES
    ctx_count = lax.axis_size("ctx")
    parts = lax.axis_size("chan") // 2
    chan_index = lax.axis_index("chan")
    place, core = chan_index // 2, chan_index % 2
    swap = [(i, i ^ 1) for i in range(2 * parts)]

    rim = shifted(featurized[tok_rows - 2 :], "ctx", 1).transpose(1, 0, 2)
    other_weight = lax.ppermute(out_weight, "chan", swap)
    features = featurized.transpose(1, 0, 2)
    scaled = residue * jnp.sqrt(-jnp.expm1(-2.0 * decay_rate))
    rate_cols = jnp.broadcast_to(decay_rate.reshape(-1, 1), (filters * modes, LANES))
    scale_cols = jnp.broadcast_to(scaled.reshape(-1, 1), (filters * modes, LANES))
    rate_rows = decay_rate.reshape(blocks, 1, LANES)
    scale_rows = scaled.reshape(blocks, 1, LANES)
    per_block = LANES // group

    square = pl.BlockSpec((LANES, LANES), lambda g: (g, 0))
    tile_spec = pl.BlockSpec((per_block, CHUNK, CHUNK), lambda g: (g, 0, 0))
    lanes_spec = pl.BlockSpec((tok_rows, LANES), lambda g: (0, g))
    rim_spec = pl.BlockSpec((streams, 2, LANES), lambda g: (0, 0, g))
    taps_spec = pl.BlockSpec((3, streams, LANES), lambda g: (0, 0, g))
    state_spec = pl.BlockSpec((group, LANES), lambda g: (g, 0))

    def stream_spec(i):
        return pl.BlockSpec((1, tok_rows, LANES), lambda g: (i, 0, g))

    tiles = pl.pallas_call(
        functools.partial(toeplitz_kernel, modes),
        grid=(blocks,),
        in_specs=[square, square],
        out_specs=tile_spec,
        out_shape=jax.ShapeDtypeStruct((filters, CHUNK, CHUNK), BF16),
        compiler_params=params(),
        cost_estimate=cost(filters * CHUNK * CHUNK * 40, filters * CHUNK * CHUNK * 4),
        name="toeplitz",
    )(rate_cols, scale_cols)

    stage_shape = pltpu.VMEM((8 + tok_rows, LANES), F32)
    wide = jax.ShapeDtypeStruct((tok_rows, channels), BF16)
    gated, starts, state = pl.pallas_call(
        functools.partial(gate_kernel, modes, group),
        grid=(blocks,),
        in_specs=[stream_spec(1), stream_spec(2), rim_spec, taps_spec, square],
        out_specs=[lanes_spec, pl.BlockSpec((parts, group, LANES), lambda g: (0, g, 0)), state_spec],
        out_shape=[
            wide,
            jax.ShapeDtypeStruct((parts, blocks * group, LANES), BF16),
            jax.ShapeDtypeStruct((blocks * group, LANES), BF16),
        ],
        scratch_shapes=[stage_shape, stage_shape],
        compiler_params=params(),
        cost_estimate=cost(tok_rows * channels * 256, tok_rows * channels * 6),
        name="gate",
    )(features, features, rim, short_filter, rate_cols)

    pieces = [shifted(state, "ctx", d) for d in range(1, ctx_count)]

    row_spec = pl.BlockSpec((1, 1, LANES), lambda g, at: (g, 0, 0))
    size = tok_rows // (2 * parts)
    tail = 16

    def convolve(source, window, rows, *earlier):
        spans = rows // tail
        window_spec = pl.BlockSpec((rows, LANES), lambda g, at: (at[0], g))
        return pl.pallas_call(
            functools.partial(near_kernel, modes, group),
            grid_spec=pltpu.PrefetchScalarGridSpec(
                num_scalar_prefetch=1,
                grid=(blocks,),
                in_specs=[
                    window_spec,
                    pl.BlockSpec((1, group, LANES), lambda g, at: (at[0], g, 0)),
                    pl.BlockSpec((per_block, CHUNK, CHUNK), lambda g, at: (g, 0, 0)),
                    pl.BlockSpec((1, rows, LANES), lambda g, at: (0, at[0], g)),
                    pl.BlockSpec((1, tail, LANES), lambda g, at: (0, jnp.maximum(at[0] * spans - 1, 0), g)),
                    pl.BlockSpec((streams, 2, LANES), lambda g, at: (0, 0, g)),
                    pl.BlockSpec((3, streams, LANES), lambda g, at: (0, 0, g)),
                    pl.BlockSpec((1, LANES), lambda g, at: (0, g)),
                    row_spec,
                    row_spec,
                ]
                + [pl.BlockSpec(memory_space=pl.ANY)] * len(earlier),
                out_specs=[pl.BlockSpec((rows, LANES), lambda g, at: (0, g))] * 2,
                scratch_shapes=[
                    pltpu.VMEM((8 + rows, LANES), F32),
                    pltpu.VMEM((rows // CHUNK, LANES, CHUNK), BF16),
                    pltpu.VMEM((rows // CHUNK, LANES, CHUNK), BF16),
                ],
            ),
            out_shape=[jax.ShapeDtypeStruct((rows, channels), BF16)] * 2,
            compiler_params=params(),
            cost_estimate=cost(rows * channels * 1024, rows * channels * 8),
            name="near",
        )(
            window.reshape(1).astype(jnp.int32),
            source,
            starts,
            tiles,
            features,
            features,
            rim,
            short_filter,
            skip_gain.reshape(1, channels),
            rate_rows,
            scale_rows,
            *earlier,
        )

    def finish(near, query, window):
        rows = near.shape[0]
        held = rows // (2 * size)
        out_spec = pl.BlockSpec((held, size, LANES), lambda g, at: (0, 0, g))
        return pl.pallas_call(
            functools.partial(mix_kernel, modes, group, tok_rows, size),
            grid_spec=pltpu.PrefetchScalarGridSpec(
                num_scalar_prefetch=1,
                grid=(blocks,),
                in_specs=[pl.BlockSpec((rows, LANES), lambda g, at: (0, g))] * 2
                + [pl.BlockSpec((group, LANES), lambda g, at: (g, 0))] * len(pieces)
                + [row_spec, row_spec],
                out_specs=[out_spec, out_spec],
                scratch_shapes=[pltpu.VMEM((2, held, size, LANES), BF16)],
            ),
            out_shape=[jax.ShapeDtypeStruct((held, size, channels), BF16)] * 2,
            compiler_params=params(),
            cost_estimate=cost(rows * channels * 256, rows * channels * 8),
            name="mix",
        )(jnp.stack([core, window]).astype(jnp.int32), near, query, *pieces, rate_rows, scale_rows)

    nothing = core * 0
    if parts != 4:
        keep, give = finish(*convolve(gated, nothing, tok_rows), nothing)
        return sum_over_line(place, keep, lax.ppermute(give, "chan", swap), out_weight, other_weight)

    far, far_inner = jnp.where(place < 2, 3, 0), jnp.where(place < 2, 2, 1)
    close, close_inner = 3 - far, 3 - far_inner
    at_end = (place == 0) | (place == 3)
    inward, across, outward = pairs([(0, 1), (3, 2)]), pairs([(1, 2), (2, 1)]), pairs([(1, 0), (2, 3)])
    send = lambda value, hops: lax.ppermute(value, "chan", hops)

    keep, give = finish(*convolve(gated, far, tok_rows // parts), far)
    other = send(give, swap)
    first = product(nothing, keep, other, out_weight, other_weight, 0, 1)
    from_end = send(first, inward)

    keep, give = finish(*convolve(gated, nothing, tok_rows, first), nothing)
    swapped = lambda which: send(lax.dynamic_slice_in_dim(give, which, 1, 0), swap)
    multiply = lambda which, other: product(which, keep, other, out_weight, other_weight, 0, 1, nothing)
    half = out_weight.shape[1] // 2
    halves = lambda value: (value[:, :half], value[:, half:])
    second = multiply(far_inner, swapped(far_inner))
    through = send(second, inward)
    crossed = [send(value, across) for value in halves(add(first, from_end))]
    which = jnp.where(at_end, close_inner, close)
    third = multiply(which, swapped(which))
    last = send(add(third, jnp.concatenate(crossed, axis=1)), inward + outward)
    inner = [send(value, across) for value in halves(add(second, through))]
    own = multiply(place, swapped(place))
    return add(own, last, jnp.concatenate(inner, axis=1))


def solution(mesh):
    return jax.shard_map(
        on_device,
        mesh=mesh,
        in_specs=(
            P("ctx", None, "chan"),
            P(None, None, "chan"),
            P("chan", None),
            P("chan", None),
            P("chan"),
            P("chan", None),
        ),
        out_specs=P(("ctx", "chan"), None),
        check_vma=False,
    )
```

```python
import functools

import jax
import jax.numpy as jnp
from jax import lax
from jax.experimental import pallas as pl
from jax.experimental.pallas import tpu as pltpu
from jax.sharding import PartitionSpec as P

LANES = 128
CHUNK = 128
BF16 = jnp.bfloat16
F32 = jnp.float32


def params(mib=48):
    return pltpu.CompilerParams(vmem_limit_bytes=mib << 20)


def cost(flops, moved):
    return pl.CostEstimate(flops=int(flops) // 64, bytes_accessed=int(moved) // 64, transcendentals=0)


def iota(shape, dim):
    return lax.broadcasted_iota(jnp.int32, shape, dim)


def toeplitz_kernel(modes, rate_ref, scale_ref, tile_ref):
    filters = LANES // modes
    reach = iota((LANES, CHUNK), 1).astype(F32)
    terms = scale_ref[...] * jnp.exp(-rate_ref[...] * reach)
    taps = terms.reshape(filters, modes, CHUNK).sum(axis=1)
    keep = iota((CHUNK, CHUNK), 0) <= iota((CHUNK, CHUNK), 1)
    for f in range(filters):
        rows = jnp.broadcast_to(taps[f : f + 1], (CHUNK, CHUNK))
        rolled = pltpu.roll(rows, 0, 1, stride=1, stride_axis=0)
        tile_ref[f] = jnp.where(keep, rolled, 0.0).astype(BF16)


def short_conv(stream, stage_ref, x_ref, rim_ref, taps_ref, k):
    at = 8 + k * CHUNK
    return (
        taps_ref[0, stream : stream + 1, :] * stage_ref[at : at + CHUNK, :]
        + taps_ref[1, stream : stream + 1, :] * stage_ref[at - 1 : at - 1 + CHUNK, :]
        + taps_ref[2, stream : stream + 1, :] * stage_ref[at - 2 : at - 2 + CHUNK, :]
    )


def stage(stream, stage_ref, x_ref, rim_ref):
    stage_ref[0:8, :] = jnp.zeros((8, LANES), F32)
    stage_ref[6:8, :] = rim_ref[stream].astype(F32)
    stage_ref[8:, :] = x_ref[0].astype(F32)


def diagonal(modes, group):
    return (iota((LANES, LANES), 0) // modes) == (iota((LANES, LANES), 1) // group)


def dot(a, b, dims=((1,), (0,))):
    return lax.dot_general(a, b, (dims, ((), ())), preferred_element_type=F32)


def gate_kernel(
    modes, group, k_ref, v_ref, rim_ref, taps_ref, rate_ref, gated_ref, start_ref, state_ref, k_stage, v_stage
):
    stage(1, k_stage, k_ref, rim_ref)
    stage(2, v_stage, v_ref, rim_ref)
    rate = rate_ref[...]
    ends = jnp.exp(-rate * (CHUNK - 1 - iota((LANES, CHUNK), 1)).astype(F32)).astype(BF16)
    fade = jnp.exp(-rate * CHUNK)
    state = jnp.zeros((LANES, LANES), F32)
    chunks = gated_ref.shape[0] // CHUNK
    per_block = chunks // start_ref.shape[0]
    own_modes = diagonal(modes, group)
    spots = (iota((group, LANES), 0) == lax.rem(iota((group, LANES), 1), group)).astype(BF16)
    fold = lambda value: dot(spots, jnp.where(own_modes, value, 0.0).astype(BF16), ((1,), (1,))).astype(BF16)
    for k in range(chunks):
        if k % per_block == 0:
            start_ref[k // per_block] = fold(state)
        gated = (
            short_conv(1, k_stage, k_ref, rim_ref, taps_ref, k) * short_conv(2, v_stage, v_ref, rim_ref, taps_ref, k)
        ).astype(BF16)
        gated_ref[k * CHUNK : (k + 1) * CHUNK, :] = gated
        state = fade * state + dot(ends, gated)
    state_ref[...] = fold(state)


def spread(modes, group, folded):
    return jnp.where(diagonal(group, modes), jnp.concatenate([folded] * (LANES // group), axis=0), 0.0)


def near_kernel(
    modes,
    group,
    window_ref,
    gated_ref,
    start_ref,
    tile_ref,
    q_ref,
    before_ref,
    rim_ref,
    taps_ref,
    gain_ref,
    row_rate_ref,
    row_scale_ref,
    *rest,
):
    near_ref, query_ref, q_stage, sources, sums = rest[-5:]

    stage(0, q_stage, q_ref, rim_ref)

    @pl.when(window_ref[0] > 0)
    def _():
        q_stage[6:8, :] = before_ref[0].astype(F32)[before_ref.shape[1] - 2 :]

    filters = LANES // group
    chunks = gated_ref.shape[0] // CHUNK
    eye = (iota((CHUNK, CHUNK), 0) == iota((CHUNK, CHUNK), 1)).astype(BF16)
    for k in range(0, chunks, 2):
        turned = dot(eye, gated_ref[k * CHUNK : (k + 2) * CHUNK, :], ((1,), (1,))).astype(BF16)
        sources[k] = turned[:, :CHUNK]
        sources[k + 1] = turned[:, CHUNK:]
    for f in range(filters):
        rows = slice(f * group, (f + 1) * group)
        block = sources[:, rows, :].reshape(chunks * group, CHUNK)
        sums[:, rows, :] = dot(block, tile_ref[f]).astype(BF16).reshape(chunks, group, CHUNK)
    row_rate = row_rate_ref[0]
    ends = jnp.exp(-row_rate * (CHUNK - 1 - iota((CHUNK, LANES), 0)).astype(F32)).astype(BF16)
    reads = (row_scale_ref[0] * jnp.exp(-row_rate * (iota((CHUNK, LANES), 0) + 1).astype(F32))).astype(BF16)
    both = jnp.concatenate([eye, reads], axis=1)
    fade = jnp.exp(-row_rate * CHUNK)
    own_modes = diagonal(group, modes)
    gain = gain_ref[...]
    state = spread(modes, group, start_ref[0].astype(F32))
    for k in range(chunks):
        rows = slice(k * CHUNK, (k + 1) * CHUNK)
        summed = dot(both, jnp.concatenate([sums[k], state.astype(BF16)], axis=1), ((1,), (1,)))
        state = fade * state + jnp.where(own_modes, dot(sources[k], ends), 0.0)
        near_ref[rows, :] = (summed + gain * gated_ref[rows, :].astype(F32)).astype(BF16)
        query_ref[rows, :] = short_conv(0, q_stage, q_ref, rim_ref, taps_ref, k).astype(BF16)


def mix_kernel(modes, group, tok_rows, size, where_ref, near_ref, query_ref, row_rate_ref, row_scale_ref, *rest):
    keep_ref, give_ref, mixed_ref = rest[-3:]
    piece_refs = rest[: lax.axis_size("ctx") - 1]
    core = where_ref[0]
    first = (where_ref[1] * near_ref.shape[0]).astype(F32)
    row_rate = row_rate_ref[0]
    carried = jnp.zeros((group, LANES), F32)
    for d, piece_ref in enumerate(piece_refs):
        carried = carried + jnp.exp(-row_rate * float(d * tok_rows)) * piece_ref[...].astype(F32)
    state = spread(modes, group, carried).astype(BF16)
    reads = row_scale_ref[0] * jnp.exp(-row_rate * (iota((CHUNK, LANES), 0) + 1).astype(F32))
    for k in range(near_ref.shape[0] // CHUNK):
        rows = slice(k * CHUNK, (k + 1) * CHUNK)
        fade = jnp.exp(-row_rate * (first + float(k * CHUNK)))
        far = dot((reads * fade).astype(BF16), state, ((1,), (1,)))
        mixed = (query_ref[rows, :].astype(F32) * (near_ref[rows, :].astype(F32) + far)).astype(BF16)
        width = min(size, CHUNK)
        for piece in range(0, CHUNK, width):
            block, inner = divmod(k * CHUNK + piece, size)
            side = lax.rem(core + block, 2)
            mixed_ref[side, block // 2, inner : inner + width, :] = mixed[piece : piece + width]
    keep_ref[...] = mixed_ref[0]
    give_ref[...] = mixed_ref[1]


def product_kernel(which_ref, own_ref, other_ref, own_w_ref, other_w_ref, *rest):
    out_ref = rest[-1]
    out_ref[...] = (dot(own_ref[0], own_w_ref[...]) + dot(other_ref[0], other_w_ref[...])).astype(BF16)


def corner(value):
    zeros = (0,) * value.ndim
    return pl.BlockSpec((1,) * (value.ndim - 2) + (16, LANES), lambda *at: zeros)


def product(which, own, other, own_w, other_w, columns, other_which=None, earlier=()):
    _, rows, depth = own.shape
    first, stop = columns
    tile = min(1024, stop - first)
    base = first // tile
    width = stop - first
    return pl.pallas_call(
        product_kernel,
        grid_spec=pltpu.PrefetchScalarGridSpec(
            num_scalar_prefetch=1,
            grid=(width // tile,),
            in_specs=[
                pl.BlockSpec((1, rows, depth), lambda j, which: (which[0], 0, 0)),
                pl.BlockSpec((1, rows, depth), lambda j, which: (which[1], 0, 0)),
                pl.BlockSpec((depth, tile), lambda j, which: (0, base + j)),
                pl.BlockSpec((depth, tile), lambda j, which: (0, base + j)),
            ]
            + [corner(value) for value in earlier],
            out_specs=pl.BlockSpec((rows, tile), lambda j, which: (0, j)),
        ),
        out_shape=jax.ShapeDtypeStruct((rows, width), BF16),
        compiler_params=params(),
        cost_estimate=cost(4 * rows * depth * width, 4 * depth * width + 6 * rows * width),
        name="product",
    )(
        jnp.stack([which, which if other_which is None else other_which]).astype(jnp.int32),
        own,
        other,
        own_w,
        other_w,
        *earlier,
    )


def sum_kernel(count, *refs):
    refs[-1][...] = add(*(ref[...] for ref in refs[:count]))


def add_after(values, earlier):
    rows, width = values[0].shape
    tile = min(512, width)
    block = pl.BlockSpec((rows, tile), lambda j: (0, j))
    return pl.pallas_call(
        functools.partial(sum_kernel, len(values)),
        grid=(width // tile,),
        in_specs=[block] * len(values) + [corner(value) for value in earlier],
        out_specs=block,
        out_shape=jax.ShapeDtypeStruct((rows, width), BF16),
        compiler_params=params(),
        cost_estimate=cost(rows * width * len(values), rows * width * 6),
        name="sum",
    )(*values, *earlier)


def shifted(value, axis, steps):
    count = lax.axis_size(axis)
    return lax.ppermute(value, axis, [(i, i + steps) for i in range(count - steps)])


def add(*values):
    total = values[0].astype(F32)
    for value in values[1:]:
        total = total + value.astype(F32)
    return total.astype(BF16)


def pairs(hops):
    return [(2 * i + c, 2 * j + c) for i, j in hops for c in (0, 1)]


def sum_over_line(place, keep, other, out_weight, other_weight):
    parts = keep.shape[0]
    split = 2
    last = parts - 1
    width = out_weight.shape[1] // split
    multiply = lambda which, j: product(
        jnp.clip(which, 0, last), keep, other, out_weight, other_weight, (j * width, (j + 1) * width)
    )
    up = [None] * split
    down = [None] * split
    for s in range(1, parts):
        senders = range(0, min(s, last))
        up_pairs = [(2 * i + c, 2 * i + 2 + c) for i in senders for c in (0, 1)]
        down_pairs = [(2 * (last - i) + c, 2 * (last - i) - 2 + c) for i in senders for c in (0, 1)]
        for j in range(split):
            if s == 1:
                first = multiply(jnp.where(place == 0, last, 0), j)
                up[j], down[j] = first, first
            else:
                up[j] = (multiply(parts - s + place, j).astype(F32) + up[j].astype(F32)).astype(BF16)
                down[j] = (multiply(s - parts + place, j).astype(F32) + down[j].astype(F32)).astype(BF16)
            up[j] = lax.ppermute(up[j], "chan", up_pairs)
            down[j] = lax.ppermute(down[j], "chan", down_pairs)
    outs = [
        (multiply(place, j).astype(F32) + up[j].astype(F32) + down[j].astype(F32)).astype(BF16) for j in range(split)
    ]
    return jnp.concatenate(outs, axis=1)


def on_device(featurized, short_filter, decay_rate, residue, skip_gain, out_weight):
    tok_rows, streams, channels = featurized.shape
    filters, modes = decay_rate.shape
    group = channels // filters
    blocks = channels // LANES
    ctx_count = lax.axis_size("ctx")
    parts = lax.axis_size("chan") // 2
    chan_index = lax.axis_index("chan")
    place, core = chan_index // 2, chan_index % 2
    swap = [(i, i ^ 1) for i in range(2 * parts)]

    rim = shifted(featurized[tok_rows - 2 :], "ctx", 1).transpose(1, 0, 2)
    other_weight = lax.ppermute(out_weight, "chan", swap)
    features = featurized.transpose(1, 0, 2)
    scaled = residue * jnp.sqrt(-jnp.expm1(-2.0 * decay_rate))
    rate_cols = jnp.broadcast_to(decay_rate.reshape(-1, 1), (filters * modes, LANES))
    scale_cols = jnp.broadcast_to(scaled.reshape(-1, 1), (filters * modes, LANES))
    rate_rows = decay_rate.reshape(blocks, 1, LANES)
    scale_rows = scaled.reshape(blocks, 1, LANES)
    per_block = LANES // group

    square = pl.BlockSpec((LANES, LANES), lambda g: (g, 0))
    tile_spec = pl.BlockSpec((per_block, CHUNK, CHUNK), lambda g: (g, 0, 0))
    lanes_spec = pl.BlockSpec((tok_rows, LANES), lambda g: (0, g))
    rim_spec = pl.BlockSpec((streams, 2, LANES), lambda g: (0, 0, g))
    taps_spec = pl.BlockSpec((3, streams, LANES), lambda g: (0, 0, g))
    state_spec = pl.BlockSpec((group, LANES), lambda g: (g, 0))

    def stream_spec(i):
        return pl.BlockSpec((1, tok_rows, LANES), lambda g: (i, 0, g))

    tiles = pl.pallas_call(
        functools.partial(toeplitz_kernel, modes),
        grid=(blocks,),
        in_specs=[square, square],
        out_specs=tile_spec,
        out_shape=jax.ShapeDtypeStruct((filters, CHUNK, CHUNK), BF16),
        compiler_params=params(),
        cost_estimate=cost(filters * CHUNK * CHUNK * 40, filters * CHUNK * CHUNK * 4),
        name="toeplitz",
    )(rate_cols, scale_cols)

    stage_shape = pltpu.VMEM((8 + tok_rows, LANES), F32)
    wide = jax.ShapeDtypeStruct((tok_rows, channels), BF16)
    gated, starts, state = pl.pallas_call(
        functools.partial(gate_kernel, modes, group),
        grid=(blocks,),
        in_specs=[stream_spec(1), stream_spec(2), rim_spec, taps_spec, square],
        out_specs=[lanes_spec, pl.BlockSpec((parts, group, LANES), lambda g: (0, g, 0)), state_spec],
        out_shape=[
            wide,
            jax.ShapeDtypeStruct((parts, blocks * group, LANES), BF16),
            jax.ShapeDtypeStruct((blocks * group, LANES), BF16),
        ],
        scratch_shapes=[stage_shape, stage_shape],
        compiler_params=params(),
        cost_estimate=cost(tok_rows * channels * 256, tok_rows * channels * 6),
        name="gate",
    )(features, features, rim, short_filter, rate_cols)

    pieces = [shifted(state, "ctx", d) for d in range(1, ctx_count)]

    row_spec = pl.BlockSpec((1, 1, LANES), lambda g, at: (g, 0, 0))
    size = tok_rows // (2 * parts)
    tail = 16

    def convolve(source, window, rows, *earlier):
        spans = rows // tail
        window_spec = pl.BlockSpec((rows, LANES), lambda g, at: (at[0], g))
        return pl.pallas_call(
            functools.partial(near_kernel, modes, group),
            grid_spec=pltpu.PrefetchScalarGridSpec(
                num_scalar_prefetch=1,
                grid=(blocks,),
                in_specs=[
                    window_spec,
                    pl.BlockSpec((1, group, LANES), lambda g, at: (at[0], g, 0)),
                    pl.BlockSpec((per_block, CHUNK, CHUNK), lambda g, at: (g, 0, 0)),
                    pl.BlockSpec((1, rows, LANES), lambda g, at: (0, at[0], g)),
                    pl.BlockSpec((1, tail, LANES), lambda g, at: (0, jnp.maximum(at[0] * spans - 1, 0), g)),
                    pl.BlockSpec((streams, 2, LANES), lambda g, at: (0, 0, g)),
                    pl.BlockSpec((3, streams, LANES), lambda g, at: (0, 0, g)),
                    pl.BlockSpec((1, LANES), lambda g, at: (0, g)),
                    row_spec,
                    row_spec,
                ]
                + [corner(value) for value in earlier],
                out_specs=[pl.BlockSpec((rows, LANES), lambda g, at: (0, g))] * 2,
                scratch_shapes=[
                    pltpu.VMEM((8 + rows, LANES), F32),
                    pltpu.VMEM((rows // CHUNK, LANES, CHUNK), BF16),
                    pltpu.VMEM((rows // CHUNK, LANES, CHUNK), BF16),
                ],
            ),
            out_shape=[jax.ShapeDtypeStruct((rows, channels), BF16)] * 2,
            compiler_params=params(),
            cost_estimate=cost(rows * channels * 1024, rows * channels * 8),
            name="near",
        )(
            window.reshape(1).astype(jnp.int32),
            source,
            starts,
            tiles,
            features,
            features,
            rim,
            short_filter,
            skip_gain.reshape(1, channels),
            rate_rows,
            scale_rows,
            *earlier,
        )

    def finish(near, query, window, *earlier):
        rows = near.shape[0]
        held = rows // (2 * size)
        out_spec = pl.BlockSpec((held, size, LANES), lambda g, at: (0, 0, g))
        return pl.pallas_call(
            functools.partial(mix_kernel, modes, group, tok_rows, size),
            grid_spec=pltpu.PrefetchScalarGridSpec(
                num_scalar_prefetch=1,
                grid=(blocks,),
                in_specs=[pl.BlockSpec((rows, LANES), lambda g, at: (0, g))] * 2
                + [row_spec, row_spec]
                + [pl.BlockSpec((group, LANES), lambda g, at: (g, 0))] * len(pieces)
                + [corner(value) for value in earlier],
                out_specs=[out_spec, out_spec],
                scratch_shapes=[pltpu.VMEM((2, held, size, LANES), BF16)],
            ),
            out_shape=[jax.ShapeDtypeStruct((held, size, channels), BF16)] * 2,
            compiler_params=params(),
            cost_estimate=cost(rows * channels * 256, rows * channels * 8),
            name="mix",
        )(jnp.stack([core, window]).astype(jnp.int32), near, query, rate_rows, scale_rows, *pieces, *earlier)

    nothing = core * 0
    if parts != 4:
        keep, give = finish(*convolve(gated, nothing, tok_rows), nothing)
        return sum_over_line(place, keep, lax.ppermute(give, "chan", swap), out_weight, other_weight)

    far, far_inner = jnp.where(place < 2, 3, 0), jnp.where(place < 2, 2, 1)
    close, close_inner = 3 - far, 3 - far_inner
    inward, across, outward = pairs([(0, 1), (3, 2)]), pairs([(1, 2), (2, 1)]), pairs([(1, 0), (2, 3)])
    send = lambda value, hops: lax.ppermute(value, "chan", hops)

    keep, give = finish(*convolve(gated, far, tok_rows // parts), far)
    other = send(give, swap)
    width = out_weight.shape[1]
    whole, even = (0, width), ((0, width // 2), (width // 2, width))
    join = lambda values: jnp.concatenate(values, axis=1)
    first = []
    for c in even:
        first.append(product(nothing, keep, other, out_weight, other_weight, c, nothing, first))
    from_end = [send(value, inward) for value in first]
    keep, give = finish(*convolve(gated, far_inner, tok_rows // parts, first[1]), far_inner)
    second = product(nothing, keep, send(give, swap), out_weight, other_weight, whole)
    through = send(second, inward)
    far_sum = [add(first[0], from_end[0])]
    crossed = [send(far_sum[0], across)]

    near, query = convolve(gated, nothing, tok_rows, second, far_sum[0])
    far_sum.append(add_after((first[1], from_end[1]), (near,)))
    crossed.append(send(far_sum[1], across))
    keep, give = finish(near, query, nothing, far_sum[1])
    swapped = lambda which: send(lax.dynamic_slice_in_dim(give, which, 1, 0), swap)
    multiply = lambda which, other, *earlier: product(
        which, keep, other, out_weight, other_weight, whole, nothing, earlier
    )
    others = [swapped(which) for which in (close_inner, close, place)]
    third = multiply(close_inner, others[0])
    last = send(third, inward)
    outer = multiply(close, others[1], third, crossed[0])
    inner_sum = add(second, through)
    inner = send(inner_sum, across)
    own = multiply(place, others[2], outer, inner_sum)
    outer = send(add(outer, join(crossed)), outward)
    return add(add(own, outer, last), inner)


def solution(mesh):
    return jax.shard_map(
        on_device,
        mesh=mesh,
        in_specs=(
            P("ctx", None, "chan"),
            P(None, None, "chan"),
            P("chan", None),
            P("chan", None),
            P("chan"),
            P("chan", None),
        ),
        out_specs=P(("ctx", "chan"), None),
        check_vma=False,
    )
```

```python
import functools

import jax
import jax.numpy as jnp
from jax import lax
from jax.experimental import pallas as pl
from jax.experimental.pallas import tpu as pltpu
from jax.sharding import PartitionSpec as P

LANES = 128
CHUNK = 128
PARTS = 2
BF16 = jnp.bfloat16
F32 = jnp.float32


def params(mib=48):
    return pltpu.CompilerParams(vmem_limit_bytes=mib << 20)


def cost(flops, moved):
    return pl.CostEstimate(flops=int(flops) // 64, bytes_accessed=int(moved) // 64, transcendentals=0)


def iota(shape, dim):
    return lax.broadcasted_iota(jnp.int32, shape, dim)


def toeplitz_kernel(modes, rate_ref, scale_ref, tile_ref):
    filters = LANES // modes
    reach = iota((LANES, CHUNK), 1).astype(F32)
    terms = scale_ref[...] * jnp.exp(-rate_ref[...] * reach)
    taps = terms.reshape(filters, modes, CHUNK).sum(axis=1)
    keep = iota((CHUNK, CHUNK), 0) <= iota((CHUNK, CHUNK), 1)
    for f in range(filters):
        rows = jnp.broadcast_to(taps[f : f + 1], (CHUNK, CHUNK))
        rolled = pltpu.roll(rows, 0, 1, stride=1, stride_axis=0)
        tile_ref[f] = jnp.where(keep, rolled, 0.0).astype(BF16)


def short_conv(stream, stage_ref, taps_ref, k):
    at = 8 + k * CHUNK
    return (
        taps_ref[0, stream : stream + 1, :] * stage_ref[at : at + CHUNK, :]
        + taps_ref[1, stream : stream + 1, :] * stage_ref[at - 1 : at - 1 + CHUNK, :]
        + taps_ref[2, stream : stream + 1, :] * stage_ref[at - 2 : at - 2 + CHUNK, :]
    )


def stage(stage_ref, x_ref, rim):
    stage_ref[0:8, :] = jnp.zeros((8, LANES), F32)
    stage_ref[6:8, :] = rim.astype(F32)
    stage_ref[8:, :] = x_ref[0].astype(F32)


def in_turns(body):
    for _ in zip(*(body(part, slice(part * LANES, (part + 1) * LANES)) for part in range(PARTS))):
        pass


def diagonal(modes, group):
    return (iota((LANES, LANES), 0) // modes) == (iota((LANES, LANES), 1) // group)


def dot(a, b, dims=((1,), (0,))):
    return lax.dot_general(a, b, (dims, ((), ())), preferred_element_type=F32)


def gate_kernel(
    modes, group, k_ref, v_ref, rim_ref, taps_ref, rate_ref, gated_ref, start_ref, state_ref, k_stages, v_stages
):
    chunks = gated_ref.shape[0] // CHUNK
    per_block = chunks // start_ref.shape[0]
    own_modes = diagonal(modes, group)
    spots = (iota((group, LANES), 0) == lax.rem(iota((group, LANES), 1), group)).astype(BF16)
    fold = lambda value: dot(spots, jnp.where(own_modes, value, 0.0).astype(BF16), ((1,), (1,))).astype(BF16)

    def body(part, lanes):
        k_stage, v_stage, taps = k_stages.at[part], v_stages.at[part], taps_ref.at[:, :, lanes]
        folded = slice(part * group, (part + 1) * group)
        stage(k_stage, k_ref.at[:, :, lanes], rim_ref[1, :, lanes])
        stage(v_stage, v_ref.at[:, :, lanes], rim_ref[2, :, lanes])
        rate = rate_ref[lanes, :]
        ends = jnp.exp(-rate * (CHUNK - 1 - iota((LANES, CHUNK), 1)).astype(F32)).astype(BF16)
        fade = jnp.exp(-rate * CHUNK)
        state = jnp.zeros((LANES, LANES), F32)
        yield
        for k in range(chunks):
            if k % per_block == 0:
                start_ref[k // per_block, folded, :] = fold(state)
            gated = (short_conv(1, k_stage, taps, k) * short_conv(2, v_stage, taps, k)).astype(BF16)
            gated_ref[k * CHUNK : (k + 1) * CHUNK, lanes] = gated
            state = fade * state + dot(ends, gated)
            yield
        state_ref[folded, :] = fold(state)
        yield

    in_turns(body)


def spread(modes, group, folded):
    return jnp.where(diagonal(group, modes), jnp.concatenate([folded] * (LANES // group), axis=0), 0.0)


def near_kernel(
    modes,
    group,
    window_ref,
    gated_ref,
    start_ref,
    tile_ref,
    q_ref,
    before_ref,
    rim_ref,
    taps_ref,
    gain_ref,
    row_rate_ref,
    row_scale_ref,
    *rest,
):
    near_ref, query_ref, q_stages, all_sources, all_sums = rest[-5:]
    filters = LANES // group
    chunks = gated_ref.shape[0] // CHUNK
    eye = (iota((CHUNK, CHUNK), 0) == iota((CHUNK, CHUNK), 1)).astype(BF16)
    own_modes = diagonal(group, modes)
    inside = window_ref[0] > 0

    def body(part, lanes):
        q_stage, sources, sums = q_stages.at[part], all_sources.at[part], all_sums.at[part]
        taps = taps_ref.at[:, :, lanes]
        before = before_ref[0, :, lanes].astype(F32)[before_ref.shape[1] - 2 :]
        stage(q_stage, q_ref.at[:, :, lanes], jnp.where(inside, before, rim_ref[0, :, lanes].astype(F32)))
        yield
        for k in range(0, chunks, 2):
            turned = dot(eye, gated_ref[k * CHUNK : (k + 2) * CHUNK, lanes], ((1,), (1,))).astype(BF16)
            sources[k] = turned[:, :CHUNK]
            sources[k + 1] = turned[:, CHUNK:]
            yield
        for f in range(filters):
            rows = slice(f * group, (f + 1) * group)
            block = sources[:, rows, :].reshape(chunks * group, CHUNK)
            sums[:, rows, :] = dot(block, tile_ref[part * filters + f]).astype(BF16).reshape(chunks, group, CHUNK)
            yield
        row_rate = row_rate_ref[part]
        ends = jnp.exp(-row_rate * (CHUNK - 1 - iota((CHUNK, LANES), 0)).astype(F32)).astype(BF16)
        reads = (row_scale_ref[part] * jnp.exp(-row_rate * (iota((CHUNK, LANES), 0) + 1).astype(F32))).astype(BF16)
        both = jnp.concatenate([eye, reads], axis=1)
        fade = jnp.exp(-row_rate * CHUNK)
        gain = gain_ref[:, lanes]
        state = spread(modes, group, start_ref[0, part * group : (part + 1) * group, :].astype(F32))
        for k in range(chunks):
            rows = slice(k * CHUNK, (k + 1) * CHUNK)
            summed = dot(both, jnp.concatenate([sums[k], state.astype(BF16)], axis=1), ((1,), (1,)))
            state = fade * state + jnp.where(own_modes, dot(sources[k], ends), 0.0)
            near_ref[rows, lanes] = (summed + gain * gated_ref[rows, lanes].astype(F32)).astype(BF16)
            query_ref[rows, lanes] = short_conv(0, q_stage, taps, k).astype(BF16)
            yield

    in_turns(body)


def mix_kernel(modes, group, tok_rows, size, where_ref, near_ref, query_ref, row_rate_ref, row_scale_ref, *rest):
    keep_ref, give_ref, mixed_ref = rest[-3:]
    piece_refs = rest[: lax.axis_size("ctx") - 1]
    core = where_ref[0]
    first = (where_ref[1] * near_ref.shape[0]).astype(F32)
    row_rate = row_rate_ref[0]
    carried = jnp.zeros((group, LANES), F32)
    for d, piece_ref in enumerate(piece_refs):
        carried = carried + jnp.exp(-row_rate * float(d * tok_rows)) * piece_ref[...].astype(F32)
    state = spread(modes, group, carried).astype(BF16)
    reads = row_scale_ref[0] * jnp.exp(-row_rate * (iota((CHUNK, LANES), 0) + 1).astype(F32))
    for k in range(near_ref.shape[0] // CHUNK):
        rows = slice(k * CHUNK, (k + 1) * CHUNK)
        fade = jnp.exp(-row_rate * (first + float(k * CHUNK)))
        far = dot((reads * fade).astype(BF16), state, ((1,), (1,)))
        mixed = (query_ref[rows, :].astype(F32) * (near_ref[rows, :].astype(F32) + far)).astype(BF16)
        width = min(size, CHUNK)
        for piece in range(0, CHUNK, width):
            block, inner = divmod(k * CHUNK + piece, size)
            side = lax.rem(core + block, 2)
            mixed_ref[side, block // 2, inner : inner + width, :] = mixed[piece : piece + width]
    keep_ref[...] = mixed_ref[0]
    give_ref[...] = mixed_ref[1]


def product_kernel(which_ref, own_ref, other_ref, own_w_ref, other_w_ref, *rest):
    out_ref = rest[-1]
    out_ref[...] = (dot(own_ref[0], own_w_ref[...]) + dot(other_ref[0], other_w_ref[...])).astype(BF16)


def corner(value):
    zeros = (0,) * value.ndim
    return pl.BlockSpec((1,) * (value.ndim - 2) + (16, LANES), lambda *at: zeros)


def product(which, own, other, own_w, other_w, columns, other_which=None, earlier=()):
    _, rows, depth = own.shape
    first, stop = columns
    tile = min(1024, stop - first)
    base = first // tile
    width = stop - first
    return pl.pallas_call(
        product_kernel,
        grid_spec=pltpu.PrefetchScalarGridSpec(
            num_scalar_prefetch=1,
            grid=(width // tile,),
            in_specs=[
                pl.BlockSpec((1, rows, depth), lambda j, which: (which[0], 0, 0)),
                pl.BlockSpec((1, rows, depth), lambda j, which: (which[1], 0, 0)),
                pl.BlockSpec((depth, tile), lambda j, which: (0, base + j)),
                pl.BlockSpec((depth, tile), lambda j, which: (0, base + j)),
            ]
            + [corner(value) for value in earlier],
            out_specs=pl.BlockSpec((rows, tile), lambda j, which: (0, j)),
        ),
        out_shape=jax.ShapeDtypeStruct((rows, width), BF16),
        compiler_params=params(),
        cost_estimate=cost(4 * rows * depth * width, 4 * depth * width + 6 * rows * width),
        name="product",
    )(
        jnp.stack([which, which if other_which is None else other_which]).astype(jnp.int32),
        own,
        other,
        own_w,
        other_w,
        *earlier,
    )


def sum_kernel(count, *refs):
    refs[-1][...] = add(*(ref[...] for ref in refs[:count]))


def add_after(values, earlier):
    rows, width = values[0].shape
    tile = min(512, width)
    block = pl.BlockSpec((rows, tile), lambda j: (0, j))
    return pl.pallas_call(
        functools.partial(sum_kernel, len(values)),
        grid=(width // tile,),
        in_specs=[block] * len(values) + [corner(value) for value in earlier],
        out_specs=block,
        out_shape=jax.ShapeDtypeStruct((rows, width), BF16),
        compiler_params=params(),
        cost_estimate=cost(rows * width * len(values), rows * width * 6),
        name="sum",
    )(*values, *earlier)


def shifted(value, axis, steps):
    count = lax.axis_size(axis)
    return lax.ppermute(value, axis, [(i, i + steps) for i in range(count - steps)])


def add(*values):
    total = values[0].astype(F32)
    for value in values[1:]:
        total = total + value.astype(F32)
    return total.astype(BF16)


def pairs(hops):
    return [(2 * i + c, 2 * j + c) for i, j in hops for c in (0, 1)]


def sum_over_line(place, keep, other, out_weight, other_weight):
    parts = keep.shape[0]
    split = 2
    last = parts - 1
    width = out_weight.shape[1] // split
    multiply = lambda which, j: product(
        jnp.clip(which, 0, last), keep, other, out_weight, other_weight, (j * width, (j + 1) * width)
    )
    up = [None] * split
    down = [None] * split
    for s in range(1, parts):
        senders = range(0, min(s, last))
        up_pairs = [(2 * i + c, 2 * i + 2 + c) for i in senders for c in (0, 1)]
        down_pairs = [(2 * (last - i) + c, 2 * (last - i) - 2 + c) for i in senders for c in (0, 1)]
        for j in range(split):
            if s == 1:
                first = multiply(jnp.where(place == 0, last, 0), j)
                up[j], down[j] = first, first
            else:
                up[j] = (multiply(parts - s + place, j).astype(F32) + up[j].astype(F32)).astype(BF16)
                down[j] = (multiply(s - parts + place, j).astype(F32) + down[j].astype(F32)).astype(BF16)
            up[j] = lax.ppermute(up[j], "chan", up_pairs)
            down[j] = lax.ppermute(down[j], "chan", down_pairs)
    outs = [
        (multiply(place, j).astype(F32) + up[j].astype(F32) + down[j].astype(F32)).astype(BF16) for j in range(split)
    ]
    return jnp.concatenate(outs, axis=1)


def on_device(featurized, short_filter, decay_rate, residue, skip_gain, out_weight):
    tok_rows, streams, channels = featurized.shape
    filters, modes = decay_rate.shape
    group = channels // filters
    blocks = channels // LANES
    ctx_count = lax.axis_size("ctx")
    parts = lax.axis_size("chan") // 2
    chan_index = lax.axis_index("chan")
    place, core = chan_index // 2, chan_index % 2
    swap = [(i, i ^ 1) for i in range(2 * parts)]

    rim = shifted(featurized[tok_rows - 2 :], "ctx", 1).transpose(1, 0, 2)
    other_weight = lax.ppermute(out_weight, "chan", swap)
    features = featurized.transpose(1, 0, 2)
    scaled = residue * jnp.sqrt(-jnp.expm1(-2.0 * decay_rate))
    rate_cols = jnp.broadcast_to(decay_rate.reshape(-1, 1), (filters * modes, LANES))
    scale_cols = jnp.broadcast_to(scaled.reshape(-1, 1), (filters * modes, LANES))
    rate_rows = decay_rate.reshape(blocks, 1, LANES)
    scale_rows = scaled.reshape(blocks, 1, LANES)
    per_block = LANES // group

    square = pl.BlockSpec((LANES, LANES), lambda g: (g, 0))
    tile_spec = pl.BlockSpec((per_block, CHUNK, CHUNK), lambda g: (g, 0, 0))
    wide_lanes = PARTS * LANES
    lanes_spec = pl.BlockSpec((tok_rows, wide_lanes), lambda g: (0, g))
    rim_spec = pl.BlockSpec((streams, 2, wide_lanes), lambda g: (0, 0, g))
    taps_spec = pl.BlockSpec((3, streams, wide_lanes), lambda g: (0, 0, g))

    def stream_spec(i):
        return pl.BlockSpec((1, tok_rows, wide_lanes), lambda g: (i, 0, g))

    tiles = pl.pallas_call(
        functools.partial(toeplitz_kernel, modes),
        grid=(blocks,),
        in_specs=[square, square],
        out_specs=tile_spec,
        out_shape=jax.ShapeDtypeStruct((filters, CHUNK, CHUNK), BF16),
        compiler_params=params(),
        cost_estimate=cost(filters * CHUNK * CHUNK * 40, filters * CHUNK * CHUNK * 4),
        name="toeplitz",
    )(rate_cols, scale_cols)

    stage_shape = pltpu.VMEM((PARTS, 8 + tok_rows, LANES), F32)
    wide = jax.ShapeDtypeStruct((tok_rows, channels), BF16)
    gated, starts, state = pl.pallas_call(
        functools.partial(gate_kernel, modes, group),
        grid=(blocks // PARTS,),
        in_specs=[
            stream_spec(1),
            stream_spec(2),
            rim_spec,
            taps_spec,
            pl.BlockSpec((wide_lanes, LANES), lambda g: (g, 0)),
        ],
        out_specs=[
            lanes_spec,
            pl.BlockSpec((parts, PARTS * group, LANES), lambda g: (0, g, 0)),
            pl.BlockSpec((PARTS * group, LANES), lambda g: (g, 0)),
        ],
        out_shape=[
            wide,
            jax.ShapeDtypeStruct((parts, blocks * group, LANES), BF16),
            jax.ShapeDtypeStruct((blocks * group, LANES), BF16),
        ],
        scratch_shapes=[stage_shape, stage_shape],
        compiler_params=params(),
        cost_estimate=cost(tok_rows * channels * 256, tok_rows * channels * 6),
        name="gate",
    )(features, features, rim, short_filter, rate_cols)

    pieces = [shifted(state, "ctx", d) for d in range(1, ctx_count)]

    row_spec = pl.BlockSpec((1, 1, LANES), lambda g, at: (g, 0, 0))
    size = tok_rows // (2 * parts)
    tail = 16

    def convolve(source, window, rows, *earlier):
        spans = rows // tail
        window_spec = pl.BlockSpec((rows, wide_lanes), lambda g, at: (at[0], g))
        rows_spec = pl.BlockSpec((PARTS, 1, LANES), lambda g, at: (g, 0, 0))
        turned_shape = pltpu.VMEM((PARTS, rows // CHUNK, LANES, CHUNK), BF16)
        return pl.pallas_call(
            functools.partial(near_kernel, modes, group),
            grid_spec=pltpu.PrefetchScalarGridSpec(
                num_scalar_prefetch=1,
                grid=(blocks // PARTS,),
                in_specs=[
                    window_spec,
                    pl.BlockSpec((1, PARTS * group, LANES), lambda g, at: (at[0], g, 0)),
                    pl.BlockSpec((PARTS * per_block, CHUNK, CHUNK), lambda g, at: (g, 0, 0)),
                    pl.BlockSpec((1, rows, wide_lanes), lambda g, at: (0, at[0], g)),
                    pl.BlockSpec((1, tail, wide_lanes), lambda g, at: (0, jnp.maximum(at[0] * spans - 1, 0), g)),
                    pl.BlockSpec((streams, 2, wide_lanes), lambda g, at: (0, 0, g)),
                    pl.BlockSpec((3, streams, wide_lanes), lambda g, at: (0, 0, g)),
                    pl.BlockSpec((1, wide_lanes), lambda g, at: (0, g)),
                    rows_spec,
                    rows_spec,
                ]
                + [corner(value) for value in earlier],
                out_specs=[pl.BlockSpec((rows, wide_lanes), lambda g, at: (0, g))] * 2,
                scratch_shapes=[pltpu.VMEM((PARTS, 8 + rows, LANES), F32), turned_shape, turned_shape],
            ),
            out_shape=[jax.ShapeDtypeStruct((rows, channels), BF16)] * 2,
            compiler_params=params(),
            cost_estimate=cost(rows * channels * 1024, rows * channels * 8),
            name="near",
        )(
            window.reshape(1).astype(jnp.int32),
            source,
            starts,
            tiles,
            features,
            features,
            rim,
            short_filter,
            skip_gain.reshape(1, channels),
            rate_rows,
            scale_rows,
            *earlier,
        )

    def finish(near, query, window, *earlier):
        rows = near.shape[0]
        held = rows // (2 * size)
        out_spec = pl.BlockSpec((held, size, LANES), lambda g, at: (0, 0, g))
        return pl.pallas_call(
            functools.partial(mix_kernel, modes, group, tok_rows, size),
            grid_spec=pltpu.PrefetchScalarGridSpec(
                num_scalar_prefetch=1,
                grid=(blocks,),
                in_specs=[pl.BlockSpec((rows, LANES), lambda g, at: (0, g))] * 2
                + [row_spec, row_spec]
                + [pl.BlockSpec((group, LANES), lambda g, at: (g, 0))] * len(pieces)
                + [corner(value) for value in earlier],
                out_specs=[out_spec, out_spec],
                scratch_shapes=[pltpu.VMEM((2, held, size, LANES), BF16)],
            ),
            out_shape=[jax.ShapeDtypeStruct((held, size, channels), BF16)] * 2,
            compiler_params=params(),
            cost_estimate=cost(rows * channels * 256, rows * channels * 8),
            name="mix",
        )(jnp.stack([core, window]).astype(jnp.int32), near, query, rate_rows, scale_rows, *pieces, *earlier)

    nothing = core * 0
    if parts != 4:
        keep, give = finish(*convolve(gated, nothing, tok_rows), nothing)
        return sum_over_line(place, keep, lax.ppermute(give, "chan", swap), out_weight, other_weight)

    far, far_inner = jnp.where(place < 2, 3, 0), jnp.where(place < 2, 2, 1)
    close, close_inner = 3 - far, 3 - far_inner
    inward, across, outward = pairs([(0, 1), (3, 2)]), pairs([(1, 2), (2, 1)]), pairs([(1, 0), (2, 3)])
    send = lambda value, hops: lax.ppermute(value, "chan", hops)

    keep, give = finish(*convolve(gated, far, tok_rows // parts), far)
    other = send(give, swap)
    width = out_weight.shape[1]
    whole, even = (0, width), ((0, width // 2), (width // 2, width))
    join = lambda values: jnp.concatenate(values, axis=1)
    first = []
    for c in even:
        first.append(product(nothing, keep, other, out_weight, other_weight, c, nothing, first))
    from_end = [send(value, inward) for value in first]
    keep, give = finish(*convolve(gated, far_inner, tok_rows // parts, first[1]), far_inner)
    second = product(nothing, keep, send(give, swap), out_weight, other_weight, whole)
    through = send(second, inward)
    far_sum = [add(first[0], from_end[0])]
    crossed = [send(far_sum[0], across)]

    near, query = convolve(gated, nothing, tok_rows, second, far_sum[0])
    far_sum.append(add_after((first[1], from_end[1]), (near,)))
    crossed.append(send(far_sum[1], across))
    keep, give = finish(near, query, nothing, far_sum[1])
    swapped = lambda which: send(lax.dynamic_slice_in_dim(give, which, 1, 0), swap)
    multiply = lambda which, other, *earlier: product(
        which, keep, other, out_weight, other_weight, whole, nothing, earlier
    )
    others = [swapped(which) for which in (close_inner, close, place)]
    third = multiply(close_inner, others[0])
    last = send(third, inward)
    outer = multiply(close, others[1], third, crossed[0])
    inner_sum = add(second, through)
    inner = send(inner_sum, across)
    own = multiply(place, others[2], outer, inner_sum)
    outer = send(add(outer, join(crossed)), outward)
    return add(add_after((own, outer, last), ()), inner)


def solution(mesh):
    return jax.shard_map(
        on_device,
        mesh=mesh,
        in_specs=(
            P("ctx", None, "chan"),
            P(None, None, "chan"),
            P("chan", None),
            P("chan", None),
            P("chan"),
            P("chan", None),
        ),
        out_specs=P(("ctx", "chan"), None),
        check_vma=False,
    )
```

```python
import functools

import jax
import jax.numpy as jnp
from jax import lax
from jax.experimental import pallas as pl
from jax.experimental.pallas import tpu as pltpu
from jax.sharding import PartitionSpec as P

LANES = 128
CHUNK = 128
PARTS = 4
BF16 = jnp.bfloat16
F32 = jnp.float32


def params(mib=48):
    return pltpu.CompilerParams(vmem_limit_bytes=mib << 20)


def cost(flops, moved):
    return pl.CostEstimate(flops=int(flops) // 64, bytes_accessed=int(moved) // 64, transcendentals=0)


def iota(shape, dim):
    return lax.broadcasted_iota(jnp.int32, shape, dim)


def toeplitz_kernel(modes, rate_ref, scale_ref, tile_ref):
    filters = LANES // modes
    reach = iota((LANES, CHUNK), 1).astype(F32)
    terms = scale_ref[...] * jnp.exp(-rate_ref[...] * reach)
    taps = terms.reshape(filters, modes, CHUNK).sum(axis=1)
    keep = iota((CHUNK, CHUNK), 0) <= iota((CHUNK, CHUNK), 1)
    for f in range(filters):
        rows = jnp.broadcast_to(taps[f : f + 1], (CHUNK, CHUNK))
        rolled = pltpu.roll(rows, 0, 1, stride=1, stride_axis=0)
        tile_ref[f] = jnp.where(keep, rolled, 0.0).astype(BF16)


def short_conv(stream, stage_ref, taps_ref, k):
    at = 8 + k * CHUNK
    return (
        taps_ref[0, stream : stream + 1, :] * stage_ref[at : at + CHUNK, :]
        + taps_ref[1, stream : stream + 1, :] * stage_ref[at - 1 : at - 1 + CHUNK, :]
        + taps_ref[2, stream : stream + 1, :] * stage_ref[at - 2 : at - 2 + CHUNK, :]
    )


def stage(stage_ref, x_ref, rim):
    stage_ref[0:8, :] = jnp.zeros((8, LANES), F32)
    stage_ref[6:8, :] = rim.astype(F32)
    stage_ref[8:, :] = x_ref[0].astype(F32)


def in_turns(body):
    for _ in zip(*(body(part, slice(part * LANES, (part + 1) * LANES)) for part in range(PARTS))):
        pass


def diagonal(modes, group):
    return (iota((LANES, LANES), 0) // modes) == (iota((LANES, LANES), 1) // group)


def dot(a, b, dims=((1,), (0,))):
    return lax.dot_general(a, b, (dims, ((), ())), preferred_element_type=F32)


def gate_kernel(
    modes, group, k_ref, v_ref, rim_ref, taps_ref, rate_ref, gated_ref, start_ref, state_ref, k_stages, v_stages
):
    chunks = gated_ref.shape[0] // CHUNK
    per_block = chunks // start_ref.shape[0]
    own_modes = diagonal(modes, group)
    spots = (iota((group, LANES), 0) == lax.rem(iota((group, LANES), 1), group)).astype(BF16)
    fold = lambda value: dot(spots, jnp.where(own_modes, value, 0.0).astype(BF16), ((1,), (1,))).astype(BF16)

    def body(part, lanes):
        k_stage, v_stage, taps = k_stages.at[part], v_stages.at[part], taps_ref.at[:, :, lanes]
        folded = slice(part * group, (part + 1) * group)
        stage(k_stage, k_ref.at[:, :, lanes], rim_ref[1, :, lanes])
        stage(v_stage, v_ref.at[:, :, lanes], rim_ref[2, :, lanes])
        rate = rate_ref[lanes, :]
        ends = jnp.exp(-rate * (CHUNK - 1 - iota((LANES, CHUNK), 1)).astype(F32)).astype(BF16)
        fade = jnp.exp(-rate * CHUNK)
        state = jnp.zeros((LANES, LANES), F32)
        yield
        for k in range(chunks):
            if k % per_block == 0:
                start_ref[k // per_block, folded, :] = fold(state)
            gated = (short_conv(1, k_stage, taps, k) * short_conv(2, v_stage, taps, k)).astype(BF16)
            gated_ref[k * CHUNK : (k + 1) * CHUNK, lanes] = gated
            state = fade * state + dot(ends, gated)
            yield
        state_ref[folded, :] = fold(state)
        yield

    in_turns(body)


def spread(modes, group, folded):
    return jnp.where(diagonal(group, modes), jnp.concatenate([folded] * (LANES // group), axis=0), 0.0)


def near_kernel(
    modes,
    group,
    window_ref,
    gated_ref,
    start_ref,
    tile_ref,
    q_ref,
    before_ref,
    rim_ref,
    taps_ref,
    gain_ref,
    row_rate_ref,
    row_scale_ref,
    *rest,
):
    near_ref, query_ref, q_stages, all_sources, all_sums = rest[-5:]
    filters = LANES // group
    chunks = gated_ref.shape[0] // CHUNK
    eye = (iota((CHUNK, CHUNK), 0) == iota((CHUNK, CHUNK), 1)).astype(BF16)
    own_modes = diagonal(group, modes)
    inside = window_ref[0] > 0

    def body(part, lanes):
        q_stage, sources, sums = q_stages.at[part], all_sources.at[part], all_sums.at[part]
        taps = taps_ref.at[:, :, lanes]
        before = before_ref[0, :, lanes].astype(F32)[before_ref.shape[1] - 2 :]
        stage(q_stage, q_ref.at[:, :, lanes], jnp.where(inside, before, rim_ref[0, :, lanes].astype(F32)))
        yield
        for k in range(0, chunks, 2):
            turned = dot(eye, gated_ref[k * CHUNK : (k + 2) * CHUNK, lanes], ((1,), (1,))).astype(BF16)
            sources[k] = turned[:, :CHUNK]
            sources[k + 1] = turned[:, CHUNK:]
            yield
        for f in range(filters):
            rows = slice(f * group, (f + 1) * group)
            block = sources[:, rows, :].reshape(chunks * group, CHUNK)
            sums[:, rows, :] = dot(block, tile_ref[part * filters + f]).astype(BF16).reshape(chunks, group, CHUNK)
            yield
        row_rate = row_rate_ref[part]
        ends = jnp.exp(-row_rate * (CHUNK - 1 - iota((CHUNK, LANES), 0)).astype(F32)).astype(BF16)
        reads = (row_scale_ref[part] * jnp.exp(-row_rate * (iota((CHUNK, LANES), 0) + 1).astype(F32))).astype(BF16)
        both = jnp.concatenate([eye, reads], axis=1)
        fade = jnp.exp(-row_rate * CHUNK)
        gain = gain_ref[:, lanes]
        state = spread(modes, group, start_ref[0, part * group : (part + 1) * group, :].astype(F32))
        for k in range(chunks):
            rows = slice(k * CHUNK, (k + 1) * CHUNK)
            summed = dot(both, jnp.concatenate([sums[k], state.astype(BF16)], axis=1), ((1,), (1,)))
            state = fade * state + jnp.where(own_modes, dot(sources[k], ends), 0.0)
            near_ref[rows, lanes] = (summed + gain * gated_ref[rows, lanes].astype(F32)).astype(BF16)
            query_ref[rows, lanes] = short_conv(0, q_stage, taps, k).astype(BF16)
            yield

    in_turns(body)


def mix_kernel(modes, group, tok_rows, size, where_ref, near_ref, query_ref, row_rate_ref, row_scale_ref, *rest):
    keep_ref, give_ref, mixed_ref = rest[-3:]
    piece_refs = rest[: lax.axis_size("ctx") - 1]
    core = where_ref[0]
    first = (where_ref[1] * near_ref.shape[0]).astype(F32)

    def body(part, lanes):
        row_rate = row_rate_ref[part]
        folded = slice(part * group, (part + 1) * group)
        carried = jnp.zeros((group, LANES), F32)
        for d, piece_ref in enumerate(piece_refs):
            carried = carried + jnp.exp(-row_rate * float(d * tok_rows)) * piece_ref[folded, :].astype(F32)
        state = spread(modes, group, carried).astype(BF16)
        reads = row_scale_ref[part] * jnp.exp(-row_rate * (iota((CHUNK, LANES), 0) + 1).astype(F32))
        yield
        for k in range(near_ref.shape[0] // CHUNK):
            rows = slice(k * CHUNK, (k + 1) * CHUNK)
            fade = jnp.exp(-row_rate * (first + float(k * CHUNK)))
            far = dot((reads * fade).astype(BF16), state, ((1,), (1,)))
            mixed = (query_ref[rows, lanes].astype(F32) * (near_ref[rows, lanes].astype(F32) + far)).astype(BF16)
            width = min(size, CHUNK)
            for piece in range(0, CHUNK, width):
                block, inner = divmod(k * CHUNK + piece, size)
                side = lax.rem(core + block, 2)
                mixed_ref[side, block // 2, inner : inner + width, lanes] = mixed[piece : piece + width]
            yield

    in_turns(body)
    keep_ref[...] = mixed_ref[0]
    give_ref[...] = mixed_ref[1]


def product_kernel(which_ref, own_ref, other_ref, own_w_ref, other_w_ref, *rest):
    out_ref = rest[-1]
    out_ref[...] = (dot(own_ref[0], own_w_ref[...]) + dot(other_ref[0], other_w_ref[...])).astype(BF16)


def corner(value):
    zeros = (0,) * value.ndim
    return pl.BlockSpec((1,) * (value.ndim - 2) + (16, LANES), lambda *at: zeros)


def product(which, own, other, own_w, other_w, columns, other_which=None, earlier=()):
    _, rows, depth = own.shape
    first, stop = columns
    tile = min(1024, stop - first)
    base = first // tile
    width = stop - first
    return pl.pallas_call(
        product_kernel,
        grid_spec=pltpu.PrefetchScalarGridSpec(
            num_scalar_prefetch=1,
            grid=(width // tile,),
            in_specs=[
                pl.BlockSpec((1, rows, depth), lambda j, which: (which[0], 0, 0)),
                pl.BlockSpec((1, rows, depth), lambda j, which: (which[1], 0, 0)),
                pl.BlockSpec((depth, tile), lambda j, which: (0, base + j)),
                pl.BlockSpec((depth, tile), lambda j, which: (0, base + j)),
            ]
            + [corner(value) for value in earlier],
            out_specs=pl.BlockSpec((rows, tile), lambda j, which: (0, j)),
        ),
        out_shape=jax.ShapeDtypeStruct((rows, width), BF16),
        compiler_params=params(),
        cost_estimate=cost(4 * rows * depth * width, 4 * depth * width + 6 * rows * width),
        name="product",
    )(
        jnp.stack([which, which if other_which is None else other_which]).astype(jnp.int32),
        own,
        other,
        own_w,
        other_w,
        *earlier,
    )


def sum_kernel(count, *refs):
    refs[-1][...] = add(*(ref[...] for ref in refs[:count]))


def add_after(values, earlier):
    rows, width = values[0].shape
    tile = min(512, width)
    block = pl.BlockSpec((rows, tile), lambda j: (0, j))
    return pl.pallas_call(
        functools.partial(sum_kernel, len(values)),
        grid=(width // tile,),
        in_specs=[block] * len(values) + [corner(value) for value in earlier],
        out_specs=block,
        out_shape=jax.ShapeDtypeStruct((rows, width), BF16),
        compiler_params=params(),
        cost_estimate=cost(rows * width * len(values), rows * width * 6),
        name="sum",
    )(*values, *earlier)


def shifted(value, axis, steps):
    count = lax.axis_size(axis)
    return lax.ppermute(value, axis, [(i, i + steps) for i in range(count - steps)])


def add(*values):
    total = values[0].astype(F32)
    for value in values[1:]:
        total = total + value.astype(F32)
    return total.astype(BF16)


def pairs(hops):
    return [(2 * i + c, 2 * j + c) for i, j in hops for c in (0, 1)]


def sum_over_line(place, keep, other, out_weight, other_weight):
    parts = keep.shape[0]
    split = 2
    last = parts - 1
    width = out_weight.shape[1] // split
    multiply = lambda which, j: product(
        jnp.clip(which, 0, last), keep, other, out_weight, other_weight, (j * width, (j + 1) * width)
    )
    up = [None] * split
    down = [None] * split
    for s in range(1, parts):
        senders = range(0, min(s, last))
        up_pairs = [(2 * i + c, 2 * i + 2 + c) for i in senders for c in (0, 1)]
        down_pairs = [(2 * (last - i) + c, 2 * (last - i) - 2 + c) for i in senders for c in (0, 1)]
        for j in range(split):
            if s == 1:
                first = multiply(jnp.where(place == 0, last, 0), j)
                up[j], down[j] = first, first
            else:
                up[j] = (multiply(parts - s + place, j).astype(F32) + up[j].astype(F32)).astype(BF16)
                down[j] = (multiply(s - parts + place, j).astype(F32) + down[j].astype(F32)).astype(BF16)
            up[j] = lax.ppermute(up[j], "chan", up_pairs)
            down[j] = lax.ppermute(down[j], "chan", down_pairs)
    outs = [
        (multiply(place, j).astype(F32) + up[j].astype(F32) + down[j].astype(F32)).astype(BF16) for j in range(split)
    ]
    return jnp.concatenate(outs, axis=1)


def on_device(featurized, short_filter, decay_rate, residue, skip_gain, out_weight):
    tok_rows, streams, channels = featurized.shape
    filters, modes = decay_rate.shape
    group = channels // filters
    blocks = channels // LANES
    ctx_count = lax.axis_size("ctx")
    parts = lax.axis_size("chan") // 2
    chan_index = lax.axis_index("chan")
    place, core = chan_index // 2, chan_index % 2
    swap = [(i, i ^ 1) for i in range(2 * parts)]

    rim = shifted(featurized[tok_rows - 2 :], "ctx", 1).transpose(1, 0, 2)
    other_weight = lax.ppermute(out_weight, "chan", swap)
    features = featurized.transpose(1, 0, 2)
    scaled = residue * jnp.sqrt(-jnp.expm1(-2.0 * decay_rate))
    rate_cols = jnp.broadcast_to(decay_rate.reshape(-1, 1), (filters * modes, LANES))
    scale_cols = jnp.broadcast_to(scaled.reshape(-1, 1), (filters * modes, LANES))
    rate_rows = decay_rate.reshape(blocks, 1, LANES)
    scale_rows = scaled.reshape(blocks, 1, LANES)
    per_block = LANES // group

    square = pl.BlockSpec((LANES, LANES), lambda g: (g, 0))
    tile_spec = pl.BlockSpec((per_block, CHUNK, CHUNK), lambda g: (g, 0, 0))
    wide_lanes = PARTS * LANES
    lanes_spec = pl.BlockSpec((tok_rows, wide_lanes), lambda g: (0, g))
    rim_spec = pl.BlockSpec((streams, 2, wide_lanes), lambda g: (0, 0, g))
    taps_spec = pl.BlockSpec((3, streams, wide_lanes), lambda g: (0, 0, g))

    def stream_spec(i):
        return pl.BlockSpec((1, tok_rows, wide_lanes), lambda g: (i, 0, g))

    tiles = pl.pallas_call(
        functools.partial(toeplitz_kernel, modes),
        grid=(blocks,),
        in_specs=[square, square],
        out_specs=tile_spec,
        out_shape=jax.ShapeDtypeStruct((filters, CHUNK, CHUNK), BF16),
        compiler_params=params(),
        cost_estimate=cost(filters * CHUNK * CHUNK * 40, filters * CHUNK * CHUNK * 4),
        name="toeplitz",
    )(rate_cols, scale_cols)

    stage_shape = pltpu.VMEM((PARTS, 8 + tok_rows, LANES), F32)
    wide = jax.ShapeDtypeStruct((tok_rows, channels), BF16)
    gated, starts, state = pl.pallas_call(
        functools.partial(gate_kernel, modes, group),
        grid=(blocks // PARTS,),
        in_specs=[
            stream_spec(1),
            stream_spec(2),
            rim_spec,
            taps_spec,
            pl.BlockSpec((wide_lanes, LANES), lambda g: (g, 0)),
        ],
        out_specs=[
            lanes_spec,
            pl.BlockSpec((parts, PARTS * group, LANES), lambda g: (0, g, 0)),
            pl.BlockSpec((PARTS * group, LANES), lambda g: (g, 0)),
        ],
        out_shape=[
            wide,
            jax.ShapeDtypeStruct((parts, blocks * group, LANES), BF16),
            jax.ShapeDtypeStruct((blocks * group, LANES), BF16),
        ],
        scratch_shapes=[stage_shape, stage_shape],
        compiler_params=params(),
        cost_estimate=cost(tok_rows * channels * 256, tok_rows * channels * 6),
        name="gate",
    )(features, features, rim, short_filter, rate_cols)

    pieces = [shifted(state, "ctx", d) for d in range(1, ctx_count)]

    row_spec = pl.BlockSpec((1, 1, LANES), lambda g, at: (g, 0, 0))
    size = tok_rows // (2 * parts)
    tail = 16

    def convolve(source, window, rows, *earlier):
        spans = rows // tail
        window_spec = pl.BlockSpec((rows, wide_lanes), lambda g, at: (at[0], g))
        rows_spec = pl.BlockSpec((PARTS, 1, LANES), lambda g, at: (g, 0, 0))
        turned_shape = pltpu.VMEM((PARTS, rows // CHUNK, LANES, CHUNK), BF16)
        return pl.pallas_call(
            functools.partial(near_kernel, modes, group),
            grid_spec=pltpu.PrefetchScalarGridSpec(
                num_scalar_prefetch=1,
                grid=(blocks // PARTS,),
                in_specs=[
                    window_spec,
                    pl.BlockSpec((1, PARTS * group, LANES), lambda g, at: (at[0], g, 0)),
                    pl.BlockSpec((PARTS * per_block, CHUNK, CHUNK), lambda g, at: (g, 0, 0)),
                    pl.BlockSpec((1, rows, wide_lanes), lambda g, at: (0, at[0], g)),
                    pl.BlockSpec((1, tail, wide_lanes), lambda g, at: (0, jnp.maximum(at[0] * spans - 1, 0), g)),
                    pl.BlockSpec((streams, 2, wide_lanes), lambda g, at: (0, 0, g)),
                    pl.BlockSpec((3, streams, wide_lanes), lambda g, at: (0, 0, g)),
                    pl.BlockSpec((1, wide_lanes), lambda g, at: (0, g)),
                    rows_spec,
                    rows_spec,
                ]
                + [corner(value) for value in earlier],
                out_specs=[pl.BlockSpec((rows, wide_lanes), lambda g, at: (0, g))] * 2,
                scratch_shapes=[pltpu.VMEM((PARTS, 8 + rows, LANES), F32), turned_shape, turned_shape],
            ),
            out_shape=[jax.ShapeDtypeStruct((rows, channels), BF16)] * 2,
            compiler_params=params(),
            cost_estimate=cost(rows * channels * 1024, rows * channels * 8),
            name="near",
        )(
            window.reshape(1).astype(jnp.int32),
            source,
            starts,
            tiles,
            features,
            features,
            rim,
            short_filter,
            skip_gain.reshape(1, channels),
            rate_rows,
            scale_rows,
            *earlier,
        )

    def finish(near, query, window, *earlier):
        rows = near.shape[0]
        held = rows // (2 * size)
        out_spec = pl.BlockSpec((held, size, wide_lanes), lambda g, at: (0, 0, g))
        rows_spec = pl.BlockSpec((PARTS, 1, LANES), lambda g, at: (g, 0, 0))
        return pl.pallas_call(
            functools.partial(mix_kernel, modes, group, tok_rows, size),
            grid_spec=pltpu.PrefetchScalarGridSpec(
                num_scalar_prefetch=1,
                grid=(blocks // PARTS,),
                in_specs=[pl.BlockSpec((rows, wide_lanes), lambda g, at: (0, g))] * 2
                + [rows_spec, rows_spec]
                + [pl.BlockSpec((PARTS * group, LANES), lambda g, at: (g, 0))] * len(pieces)
                + [corner(value) for value in earlier],
                out_specs=[out_spec, out_spec],
                scratch_shapes=[pltpu.VMEM((2, held, size, wide_lanes), BF16)],
            ),
            out_shape=[jax.ShapeDtypeStruct((held, size, channels), BF16)] * 2,
            compiler_params=params(),
            cost_estimate=cost(rows * channels * 256, rows * channels * 8),
            name="mix",
        )(jnp.stack([core, window]).astype(jnp.int32), near, query, rate_rows, scale_rows, *pieces, *earlier)

    nothing = core * 0
    if parts != 4:
        keep, give = finish(*convolve(gated, nothing, tok_rows), nothing)
        return sum_over_line(place, keep, lax.ppermute(give, "chan", swap), out_weight, other_weight)

    far, far_inner = jnp.where(place < 2, 3, 0), jnp.where(place < 2, 2, 1)
    close, close_inner = 3 - far, 3 - far_inner
    inward, across, outward = pairs([(0, 1), (3, 2)]), pairs([(1, 2), (2, 1)]), pairs([(1, 0), (2, 3)])
    send = lambda value, hops: lax.ppermute(value, "chan", hops)

    keep, give = finish(*convolve(gated, far, tok_rows // parts), far)
    other = send(give, swap)
    width = out_weight.shape[1]
    whole, even = (0, width), ((0, width // 2), (width // 2, width))
    join = lambda values: jnp.concatenate(values, axis=1)
    first = []
    for c in even:
        first.append(product(nothing, keep, other, out_weight, other_weight, c, nothing, first))
    from_end = [send(value, inward) for value in first]
    keep, give = finish(*convolve(gated, far_inner, tok_rows // parts, first[1]), far_inner)
    second = product(nothing, keep, send(give, swap), out_weight, other_weight, whole)
    through = send(second, inward)
    far_sum = [add(first[0], from_end[0])]
    crossed = [send(far_sum[0], across)]

    near, query = convolve(gated, nothing, tok_rows, second, far_sum[0])
    far_sum.append(add_after((first[1], from_end[1]), (near,)))
    crossed.append(send(far_sum[1], across))
    keep, give = finish(near, query, nothing, far_sum[1])
    swapped = lambda which: send(lax.dynamic_slice_in_dim(give, which, 1, 0), swap)
    multiply = lambda which, other, *earlier: product(
        which, keep, other, out_weight, other_weight, whole, nothing, earlier
    )
    others = [swapped(which) for which in (close_inner, close, place)]
    third = multiply(close_inner, others[0])
    last = send(third, inward)
    outer = multiply(close, others[1], third, crossed[0])
    inner_sum = add(second, through)
    inner = send(inner_sum, across)
    own = multiply(place, others[2], outer, inner_sum)
    outer = send(add(outer, join(crossed)), outward)
    return add(add_after((own, outer, last), ()), inner)


def solution(mesh):
    return jax.shard_map(
        on_device,
        mesh=mesh,
        in_specs=(
            P("ctx", None, "chan"),
            P(None, None, "chan"),
            P("chan", None),
            P("chan", None),
            P("chan"),
            P("chan", None),
        ),
        out_specs=P(("ctx", "chan"), None),
        check_vma=False,
    )
```

```python
import functools

import jax
import jax.numpy as jnp
from jax import lax
from jax.experimental import pallas as pl
from jax.experimental.pallas import tpu as pltpu
from jax.sharding import PartitionSpec as P

LANES = 128
CHUNK = 128
PARTS = 4
BF16 = jnp.bfloat16
F32 = jnp.float32


def params(mib=48):
    return pltpu.CompilerParams(vmem_limit_bytes=mib << 20)


def cost(flops, moved):
    return pl.CostEstimate(flops=int(flops) // 64, bytes_accessed=int(moved) // 64, transcendentals=0)


def iota(shape, dim):
    return lax.broadcasted_iota(jnp.int32, shape, dim)


def toeplitz_kernel(modes, rate_ref, scale_ref, tile_ref):
    filters = rate_ref.shape[0] // modes
    reach = iota(rate_ref.shape, 1).astype(F32)
    terms = scale_ref[...] * jnp.exp(-rate_ref[...] * reach)
    taps = terms.reshape(filters, modes, CHUNK).sum(axis=1)
    keep = iota((CHUNK, CHUNK), 0) <= iota((CHUNK, CHUNK), 1)
    for f in range(filters):
        rows = jnp.broadcast_to(taps[f : f + 1], (CHUNK, CHUNK))
        rolled = pltpu.roll(rows, 0, 1, stride=1, stride_axis=0)
        tile_ref[f] = jnp.where(keep, rolled, 0.0).astype(BF16)


def short_conv(stream, stage_ref, taps_ref, k):
    at = 8 + k * CHUNK
    return (
        taps_ref[0, stream : stream + 1, :] * stage_ref[at : at + CHUNK, :]
        + taps_ref[1, stream : stream + 1, :] * stage_ref[at - 1 : at - 1 + CHUNK, :]
        + taps_ref[2, stream : stream + 1, :] * stage_ref[at - 2 : at - 2 + CHUNK, :]
    )


def stage(stage_ref, x_ref, rim):
    stage_ref[0:8, :] = jnp.zeros((8, LANES), F32)
    stage_ref[6:8, :] = rim.astype(F32)
    stage_ref[8:, :] = x_ref[0].astype(F32)


def in_turns(body):
    for _ in zip(*(body(part, slice(part * LANES, (part + 1) * LANES)) for part in range(PARTS))):
        pass


def diagonal(modes, group):
    return (iota((LANES, LANES), 0) // modes) == (iota((LANES, LANES), 1) // group)


def dot(a, b, dims=((1,), (0,))):
    return lax.dot_general(a, b, (dims, ((), ())), preferred_element_type=F32)


def gate_kernel(
    modes, group, k_ref, v_ref, rim_ref, taps_ref, rate_ref, gated_ref, start_ref, state_ref, k_stages, v_stages
):
    chunks = gated_ref.shape[0] // CHUNK
    per_block = chunks // start_ref.shape[0]
    own_modes = diagonal(modes, group)
    spots = (iota((group, LANES), 0) == lax.rem(iota((group, LANES), 1), group)).astype(BF16)
    fold = lambda value: dot(spots, jnp.where(own_modes, value, 0.0).astype(BF16), ((1,), (1,))).astype(BF16)

    def body(part, lanes):
        k_stage, v_stage, taps = k_stages.at[part], v_stages.at[part], taps_ref.at[:, :, lanes]
        folded = slice(part * group, (part + 1) * group)
        stage(k_stage, k_ref.at[:, :, lanes], rim_ref[1, :, lanes])
        stage(v_stage, v_ref.at[:, :, lanes], rim_ref[2, :, lanes])
        rate = rate_ref[lanes, :]
        ends = jnp.exp(-rate * (CHUNK - 1 - iota((LANES, CHUNK), 1)).astype(F32)).astype(BF16)
        fade = jnp.exp(-rate * CHUNK)
        state = jnp.zeros((LANES, LANES), F32)
        yield
        for k in range(chunks):
            if k % per_block == 0:
                start_ref[k // per_block, folded, :] = fold(state)
            gated = (short_conv(1, k_stage, taps, k) * short_conv(2, v_stage, taps, k)).astype(BF16)
            gated_ref[k * CHUNK : (k + 1) * CHUNK, lanes] = gated
            state = fade * state + dot(ends, gated)
            yield
        state_ref[folded, :] = fold(state)
        yield

    in_turns(body)


def spread(modes, group, folded):
    return jnp.where(diagonal(group, modes), jnp.concatenate([folded] * (LANES // group), axis=0), 0.0)


def near_kernel(
    modes,
    group,
    window_ref,
    gated_ref,
    start_ref,
    tile_ref,
    q_ref,
    before_ref,
    rim_ref,
    taps_ref,
    gain_ref,
    row_rate_ref,
    row_scale_ref,
    *rest,
):
    near_ref, query_ref, q_stages, all_sources, all_sums = rest[-5:]
    filters = LANES // group
    chunks = gated_ref.shape[0] // CHUNK
    eye = (iota((CHUNK, CHUNK), 0) == iota((CHUNK, CHUNK), 1)).astype(BF16)
    own_modes = diagonal(group, modes)
    inside = window_ref[0] > 0

    def body(part, lanes):
        q_stage, sources, sums = q_stages.at[part], all_sources.at[part], all_sums.at[part]
        taps = taps_ref.at[:, :, lanes]
        before = before_ref[0, :, lanes].astype(F32)[before_ref.shape[1] - 2 :]
        stage(q_stage, q_ref.at[:, :, lanes], jnp.where(inside, before, rim_ref[0, :, lanes].astype(F32)))
        yield
        for k in range(0, chunks, 2):
            turned = dot(eye, gated_ref[k * CHUNK : (k + 2) * CHUNK, lanes], ((1,), (1,))).astype(BF16)
            sources[k] = turned[:, :CHUNK]
            sources[k + 1] = turned[:, CHUNK:]
            yield
        for f in range(filters):
            rows = slice(f * group, (f + 1) * group)
            block = sources[:, rows, :].reshape(chunks * group, CHUNK)
            sums[:, rows, :] = dot(block, tile_ref[part * filters + f]).astype(BF16).reshape(chunks, group, CHUNK)
            yield
        row_rate = row_rate_ref[part]
        ends = jnp.exp(-row_rate * (CHUNK - 1 - iota((CHUNK, LANES), 0)).astype(F32)).astype(BF16)
        reads = (row_scale_ref[part] * jnp.exp(-row_rate * (iota((CHUNK, LANES), 0) + 1).astype(F32))).astype(BF16)
        both = jnp.concatenate([eye, reads], axis=1)
        fade = jnp.exp(-row_rate * CHUNK)
        gain = gain_ref[:, lanes]
        state = spread(modes, group, start_ref[0, part * group : (part + 1) * group, :].astype(F32))
        for k in range(chunks):
            rows = slice(k * CHUNK, (k + 1) * CHUNK)
            summed = dot(both, jnp.concatenate([sums[k], state.astype(BF16)], axis=1), ((1,), (1,)))
            state = fade * state + jnp.where(own_modes, dot(sources[k], ends), 0.0)
            near_ref[rows, lanes] = (summed + gain * gated_ref[rows, lanes].astype(F32)).astype(BF16)
            query_ref[rows, lanes] = short_conv(0, q_stage, taps, k).astype(BF16)
            yield

    in_turns(body)


def mix_kernel(modes, group, tok_rows, size, where_ref, near_ref, query_ref, row_rate_ref, row_scale_ref, *rest):
    keep_ref, give_ref, mixed_ref = rest[-3:]
    piece_refs = rest[: lax.axis_size("ctx") - 1]
    core = where_ref[0]
    first = (where_ref[1] * near_ref.shape[0]).astype(F32)

    def body(part, lanes):
        row_rate = row_rate_ref[part]
        folded = slice(part * group, (part + 1) * group)
        carried = jnp.zeros((group, LANES), F32)
        for d, piece_ref in enumerate(piece_refs):
            carried = carried + jnp.exp(-row_rate * float(d * tok_rows)) * piece_ref[folded, :].astype(F32)
        state = spread(modes, group, carried).astype(BF16)
        reads = row_scale_ref[part] * jnp.exp(-row_rate * (iota((CHUNK, LANES), 0) + 1).astype(F32))
        yield
        for k in range(near_ref.shape[0] // CHUNK):
            rows = slice(k * CHUNK, (k + 1) * CHUNK)
            fade = jnp.exp(-row_rate * (first + float(k * CHUNK)))
            far = dot((reads * fade).astype(BF16), state, ((1,), (1,)))
            mixed = (query_ref[rows, lanes].astype(F32) * (near_ref[rows, lanes].astype(F32) + far)).astype(BF16)
            width = min(size, CHUNK)
            for piece in range(0, CHUNK, width):
                block, inner = divmod(k * CHUNK + piece, size)
                side = lax.rem(core + block, 2)
                mixed_ref[side, block // 2, inner : inner + width, lanes] = mixed[piece : piece + width]
            yield

    in_turns(body)
    keep_ref[...] = mixed_ref[0]
    give_ref[...] = mixed_ref[1]


def product_kernel(which_ref, own_ref, other_ref, own_w_ref, other_w_ref, *rest):
    out_ref = rest[-1]
    out_ref[...] = (dot(own_ref[0], own_w_ref[...]) + dot(other_ref[0], other_w_ref[...])).astype(BF16)


def corner(value):
    zeros = (0,) * value.ndim
    return pl.BlockSpec((1,) * (value.ndim - 2) + (16, LANES), lambda *at: zeros)


def product(which, own, other, own_w, other_w, columns, other_which=None, earlier=()):
    _, rows, depth = own.shape
    first, stop = columns
    tile = min(1024, stop - first)
    base = first // tile
    width = stop - first
    return pl.pallas_call(
        product_kernel,
        grid_spec=pltpu.PrefetchScalarGridSpec(
            num_scalar_prefetch=1,
            grid=(width // tile,),
            in_specs=[
                pl.BlockSpec((1, rows, depth), lambda j, which: (which[0], 0, 0)),
                pl.BlockSpec((1, rows, depth), lambda j, which: (which[1], 0, 0)),
                pl.BlockSpec((depth, tile), lambda j, which: (0, base + j)),
                pl.BlockSpec((depth, tile), lambda j, which: (0, base + j)),
            ]
            + [corner(value) for value in earlier],
            out_specs=pl.BlockSpec((rows, tile), lambda j, which: (0, j)),
        ),
        out_shape=jax.ShapeDtypeStruct((rows, width), BF16),
        compiler_params=params(),
        cost_estimate=cost(4 * rows * depth * width, 4 * depth * width + 6 * rows * width),
        name="product",
    )(
        jnp.stack([which, which if other_which is None else other_which]).astype(jnp.int32),
        own,
        other,
        own_w,
        other_w,
        *earlier,
    )


def sum_kernel(count, *refs):
    refs[-1][...] = add(*(ref[...] for ref in refs[:count]))


def add_after(values, earlier):
    rows, width = values[0].shape
    tile = min(512, width)
    block = pl.BlockSpec((rows, tile), lambda j: (0, j))
    return pl.pallas_call(
        functools.partial(sum_kernel, len(values)),
        grid=(width // tile,),
        in_specs=[block] * len(values) + [corner(value) for value in earlier],
        out_specs=block,
        out_shape=jax.ShapeDtypeStruct((rows, width), BF16),
        compiler_params=params(),
        cost_estimate=cost(rows * width * len(values), rows * width * 6),
        name="sum",
    )(*values, *earlier)


def shifted(value, axis, steps):
    count = lax.axis_size(axis)
    return lax.ppermute(value, axis, [(i, i + steps) for i in range(count - steps)])


def add(*values):
    total = values[0].astype(F32)
    for value in values[1:]:
        total = total + value.astype(F32)
    return total.astype(BF16)


def pairs(hops):
    return [(2 * i + c, 2 * j + c) for i, j in hops for c in (0, 1)]


def sum_over_line(place, keep, other, out_weight, other_weight):
    parts = keep.shape[0]
    split = 2
    last = parts - 1
    width = out_weight.shape[1] // split
    multiply = lambda which, j: product(
        jnp.clip(which, 0, last), keep, other, out_weight, other_weight, (j * width, (j + 1) * width)
    )
    up = [None] * split
    down = [None] * split
    for s in range(1, parts):
        senders = range(0, min(s, last))
        up_pairs = [(2 * i + c, 2 * i + 2 + c) for i in senders for c in (0, 1)]
        down_pairs = [(2 * (last - i) + c, 2 * (last - i) - 2 + c) for i in senders for c in (0, 1)]
        for j in range(split):
            if s == 1:
                first = multiply(jnp.where(place == 0, last, 0), j)
                up[j], down[j] = first, first
            else:
                up[j] = (multiply(parts - s + place, j).astype(F32) + up[j].astype(F32)).astype(BF16)
                down[j] = (multiply(s - parts + place, j).astype(F32) + down[j].astype(F32)).astype(BF16)
            up[j] = lax.ppermute(up[j], "chan", up_pairs)
            down[j] = lax.ppermute(down[j], "chan", down_pairs)
    outs = [
        (multiply(place, j).astype(F32) + up[j].astype(F32) + down[j].astype(F32)).astype(BF16) for j in range(split)
    ]
    return jnp.concatenate(outs, axis=1)


def on_device(featurized, short_filter, decay_rate, residue, skip_gain, out_weight):
    tok_rows, streams, channels = featurized.shape
    filters, modes = decay_rate.shape
    group = channels // filters
    blocks = channels // LANES
    ctx_count = lax.axis_size("ctx")
    parts = lax.axis_size("chan") // 2
    chan_index = lax.axis_index("chan")
    place, core = chan_index // 2, chan_index % 2
    swap = [(i, i ^ 1) for i in range(2 * parts)]

    rim = shifted(featurized[tok_rows - 2 :], "ctx", 1).transpose(1, 0, 2)
    other_weight = lax.ppermute(out_weight, "chan", swap)
    features = featurized.transpose(1, 0, 2)
    scaled = residue * jnp.sqrt(-jnp.expm1(-2.0 * decay_rate))
    rate_cols = jnp.broadcast_to(decay_rate.reshape(-1, 1), (filters * modes, LANES))
    scale_cols = jnp.broadcast_to(scaled.reshape(-1, 1), (filters * modes, LANES))
    rate_rows = decay_rate.reshape(blocks, 1, LANES)
    scale_rows = scaled.reshape(blocks, 1, LANES)
    per_block = LANES // group

    square = pl.BlockSpec((PARTS * LANES, LANES), lambda g: (g, 0))
    tile_spec = pl.BlockSpec((PARTS * per_block, CHUNK, CHUNK), lambda g: (g, 0, 0))
    wide_lanes = PARTS * LANES
    lanes_spec = pl.BlockSpec((tok_rows, wide_lanes), lambda g: (0, g))
    rim_spec = pl.BlockSpec((streams, 2, wide_lanes), lambda g: (0, 0, g))
    taps_spec = pl.BlockSpec((3, streams, wide_lanes), lambda g: (0, 0, g))

    def stream_spec(i):
        return pl.BlockSpec((1, tok_rows, wide_lanes), lambda g: (i, 0, g))

    tiles = pl.pallas_call(
        functools.partial(toeplitz_kernel, modes),
        grid=(blocks // PARTS,),
        in_specs=[square, square],
        out_specs=tile_spec,
        out_shape=jax.ShapeDtypeStruct((filters, CHUNK, CHUNK), BF16),
        compiler_params=params(),
        cost_estimate=cost(filters * CHUNK * CHUNK * 40, filters * CHUNK * CHUNK * 4),
        name="toeplitz",
    )(rate_cols, scale_cols)

    stage_shape = pltpu.VMEM((PARTS, 8 + tok_rows, LANES), F32)
    wide = jax.ShapeDtypeStruct((tok_rows, channels), BF16)
    gated, starts, state = pl.pallas_call(
        functools.partial(gate_kernel, modes, group),
        grid=(blocks // PARTS,),
        in_specs=[
            stream_spec(1),
            stream_spec(2),
            rim_spec,
            taps_spec,
            pl.BlockSpec((wide_lanes, LANES), lambda g: (g, 0)),
        ],
        out_specs=[
            lanes_spec,
            pl.BlockSpec((parts, PARTS * group, LANES), lambda g: (0, g, 0)),
            pl.BlockSpec((PARTS * group, LANES), lambda g: (g, 0)),
        ],
        out_shape=[
            wide,
            jax.ShapeDtypeStruct((parts, blocks * group, LANES), BF16),
            jax.ShapeDtypeStruct((blocks * group, LANES), BF16),
        ],
        scratch_shapes=[stage_shape, stage_shape],
        compiler_params=params(),
        cost_estimate=cost(tok_rows * channels * 256, tok_rows * channels * 6),
        name="gate",
    )(features, features, rim, short_filter, rate_cols)

    pieces = [shifted(state, "ctx", d) for d in range(1, ctx_count)]

    row_spec = pl.BlockSpec((1, 1, LANES), lambda g, at: (g, 0, 0))
    size = tok_rows // (2 * parts)
    tail = 16

    def convolve(source, window, rows, *earlier):
        spans = rows // tail
        window_spec = pl.BlockSpec((rows, wide_lanes), lambda g, at: (at[0], g))
        rows_spec = pl.BlockSpec((PARTS, 1, LANES), lambda g, at: (g, 0, 0))
        turned_shape = pltpu.VMEM((PARTS, rows // CHUNK, LANES, CHUNK), BF16)
        return pl.pallas_call(
            functools.partial(near_kernel, modes, group),
            grid_spec=pltpu.PrefetchScalarGridSpec(
                num_scalar_prefetch=1,
                grid=(blocks // PARTS,),
                in_specs=[
                    window_spec,
                    pl.BlockSpec((1, PARTS * group, LANES), lambda g, at: (at[0], g, 0)),
                    pl.BlockSpec((PARTS * per_block, CHUNK, CHUNK), lambda g, at: (g, 0, 0)),
                    pl.BlockSpec((1, rows, wide_lanes), lambda g, at: (0, at[0], g)),
                    pl.BlockSpec((1, tail, wide_lanes), lambda g, at: (0, jnp.maximum(at[0] * spans - 1, 0), g)),
                    pl.BlockSpec((streams, 2, wide_lanes), lambda g, at: (0, 0, g)),
                    pl.BlockSpec((3, streams, wide_lanes), lambda g, at: (0, 0, g)),
                    pl.BlockSpec((1, wide_lanes), lambda g, at: (0, g)),
                    rows_spec,
                    rows_spec,
                ]
                + [corner(value) for value in earlier],
                out_specs=[pl.BlockSpec((rows, wide_lanes), lambda g, at: (0, g))] * 2,
                scratch_shapes=[pltpu.VMEM((PARTS, 8 + rows, LANES), F32), turned_shape, turned_shape],
            ),
            out_shape=[jax.ShapeDtypeStruct((rows, channels), BF16)] * 2,
            compiler_params=params(),
            cost_estimate=cost(rows * channels * 1024, rows * channels * 8),
            name="near",
        )(
            window.reshape(1).astype(jnp.int32),
            source,
            starts,
            tiles,
            features,
            features,
            rim,
            short_filter,
            skip_gain.reshape(1, channels),
            rate_rows,
            scale_rows,
            *earlier,
        )

    def finish(near, query, window, *earlier):
        rows = near.shape[0]
        held = rows // (2 * size)
        out_spec = pl.BlockSpec((held, size, wide_lanes), lambda g, at: (0, 0, g))
        rows_spec = pl.BlockSpec((PARTS, 1, LANES), lambda g, at: (g, 0, 0))
        return pl.pallas_call(
            functools.partial(mix_kernel, modes, group, tok_rows, size),
            grid_spec=pltpu.PrefetchScalarGridSpec(
                num_scalar_prefetch=1,
                grid=(blocks // PARTS,),
                in_specs=[pl.BlockSpec((rows, wide_lanes), lambda g, at: (0, g))] * 2
                + [rows_spec, rows_spec]
                + [pl.BlockSpec((PARTS * group, LANES), lambda g, at: (g, 0))] * len(pieces)
                + [corner(value) for value in earlier],
                out_specs=[out_spec, out_spec],
                scratch_shapes=[pltpu.VMEM((2, held, size, wide_lanes), BF16)],
            ),
            out_shape=[jax.ShapeDtypeStruct((held, size, channels), BF16)] * 2,
            compiler_params=params(),
            cost_estimate=cost(rows * channels * 256, rows * channels * 8),
            name="mix",
        )(jnp.stack([core, window]).astype(jnp.int32), near, query, rate_rows, scale_rows, *pieces, *earlier)

    nothing = core * 0
    if parts != 4:
        keep, give = finish(*convolve(gated, nothing, tok_rows), nothing)
        return sum_over_line(place, keep, lax.ppermute(give, "chan", swap), out_weight, other_weight)

    far, far_inner = jnp.where(place < 2, 3, 0), jnp.where(place < 2, 2, 1)
    close, close_inner = 3 - far, 3 - far_inner
    inward, across, outward = pairs([(0, 1), (3, 2)]), pairs([(1, 2), (2, 1)]), pairs([(1, 0), (2, 3)])
    send = lambda value, hops: lax.ppermute(value, "chan", hops)

    keep, give = finish(*convolve(gated, far, tok_rows // parts), far)
    other = send(give, swap)
    width = out_weight.shape[1]
    whole, even = (0, width), ((0, width // 2), (width // 2, width))
    join = lambda values: jnp.concatenate(values, axis=1)
    first = []
    for c in even:
        first.append(product(nothing, keep, other, out_weight, other_weight, c, nothing, first))
    from_end = [send(value, inward) for value in first]
    keep, give = finish(*convolve(gated, far_inner, tok_rows // parts, first[1]), far_inner)
    second = product(nothing, keep, send(give, swap), out_weight, other_weight, whole)
    through = send(second, inward)
    far_sum = [add(first[0], from_end[0])]
    crossed = [send(far_sum[0], across)]

    near, query = convolve(gated, nothing, tok_rows, second, far_sum[0])
    far_sum.append(add_after((first[1], from_end[1]), (near,)))
    crossed.append(send(far_sum[1], across))
    keep, give = finish(near, query, nothing, far_sum[1])
    swapped = lambda which: send(lax.dynamic_slice_in_dim(give, which, 1, 0), swap)
    multiply = lambda which, other, *earlier: product(
        which, keep, other, out_weight, other_weight, whole, nothing, earlier
    )
    others = [swapped(which) for which in (close_inner, close, place)]
    third = multiply(close_inner, others[0])
    last = send(third, inward)
    outer = multiply(close, others[1], third, crossed[0])
    inner_sum = add(second, through)
    inner = send(inner_sum, across)
    own = multiply(place, others[2], outer, inner_sum)
    outer = send(add(outer, join(crossed)), outward)
    return add(add_after((own, outer, last), ()), inner)


def solution(mesh):
    return jax.shard_map(
        on_device,
        mesh=mesh,
        in_specs=(
            P("ctx", None, "chan"),
            P(None, None, "chan"),
            P("chan", None),
            P("chan", None),
            P("chan"),
            P("chan", None),
        ),
        out_specs=P(("ctx", "chan"), None),
        check_vma=False,
    )
```
